256 devices in a mesh: seq: 32 (over y_lo, z, core), head: 8 (over y_hi, x).
Axes of the slice: x: 4, y: 4 (y_hi: 2, y_lo: 2; y = y_hi * 2 + y_lo), z: 8, core: 2. Of those that a mesh axis runs over, the one named last changes fastest.
Arguments:
- teacher: bfloat16 [1, 8192, 4096], P(None, 'seq', 'head'), may hold values from -32 to 32
- student: bfloat16 [1, 8192, 1792], P(None, 'seq', 'head'), may hold values from -32 to 32
- weights: float32 [8192], P('seq'), may hold values from 1 to 32
Outputs:
- mean_loss: float32 [], replicated
- student_grad: float32 [1, 8192, 1792], P(None, 'seq', 'head')
The draws below stay inside these ranges and needn't reach their ends.
All inputs are finite; a program needn't handle non-finite values.
Results may differ from the reference program's by a relative error of at most 0.0011.
Values may be sent and summed in bfloat16 or wider, within the bound.
No kernel may reach another device: no remote copies, remote signals or barrier semaphores. Data moves between devices by JAX's collectives and lax.ppermute only.
A program may use at most 128 MiB of HBM per device.

```python
import math
import jax
import jax.numpy as jnp
from jax import lax

TW = 256
SW = 112
HEADS = 16
RELS = 1
TOKENS = 8192


def clustered_base(key, salt, head_size):
    noise_key = jax.random.fold_in(key, salt)
    assign = jax.random.randint(jax.random.fold_in(key, 5), (RELS, TOKENS, HEADS), 0, 16)
    one_hot = (assign[..., None] == jnp.arange(16, dtype=jnp.int32)).astype(jnp.float32)
    centres = jnp.clip(jax.random.normal(jax.random.fold_in(noise_key, 21), (RELS, HEADS, 16, head_size), jnp.float32), -4.0, 4.0)
    placed = jnp.einsum('rthc,rhcd->rthd', one_hot, centres)
    noise = jnp.clip(jax.random.normal(jax.random.fold_in(noise_key, 1), (RELS, TOKENS, HEADS, head_size), jnp.float32), -4.0, 4.0)
    return (0.9 * placed + 0.45 * noise).reshape(RELS, TOKENS, HEADS * head_size)


def relation_vectors(key, salt, head_size):
    base = clustered_base(key, salt, head_size)
    values = jnp.clip(base * math.sqrt(0.5), -32.0, 32.0)
    return values.astype(jnp.bfloat16)


def draw_teacher(key, part):
    return relation_vectors(key, 11, TW)


def draw_student(key, part):
    return relation_vectors(key, 13, SW)


def draw_weights(key, part):
    position = jnp.arange(TOKENS, dtype=jnp.float32) / TOKENS
    return (1.0 + 3.0 * position) * jnp.exp(jax.random.uniform(key, (TOKENS,), jnp.float32, math.log(2.0), math.log(6.0)))


def setup_inputs(seed: int = 0) -> dict:
    keys = jax.random.split(jax.random.key(seed), 4)
    teacher = draw_teacher(jax.random.fold_in(keys[3], 71), 0)
    student = draw_student(jax.random.fold_in(keys[3], 71), 0)
    weights = draw_weights(jax.random.fold_in(keys[3], 71), 0)
    return dict(teacher=teacher, student=student, weights=weights)


def relation_pair(teach_rows, stud_rows, weights):
    teach_score = jnp.dot(teach_rows, teach_rows.T, preferred_element_type=jnp.float32) * (1.0 / math.sqrt(TW))
    stud_score = jnp.dot(stud_rows, stud_rows.T, preferred_element_type=jnp.float32) * (1.0 / math.sqrt(SW))
    teach_norm = jax.nn.logsumexp(teach_score, axis=1)
    stud_norm = jax.nn.logsumexp(stud_score, axis=1)
    teach_prob = jnp.exp(teach_score - teach_norm[:, None])
    stud_prob = jnp.exp(stud_score - stud_norm[:, None])
    divergence = lax.optimization_barrier(jnp.sum(teach_prob * (teach_score - stud_score), axis=1)) - teach_norm + stud_norm
    slopes = weights[:, None] * (stud_prob - teach_prob)
    slope_mix = (slopes + slopes.T).astype(jnp.bfloat16)
    gradient = jnp.dot(slope_mix, stud_rows, preferred_element_type=jnp.float32) * (1.0 / math.sqrt(SW))
    return (jnp.sum(weights * divergence), gradient)

def reference(teacher, student, weights):
    teach_heads = teacher.reshape(RELS, TOKENS, HEADS, TW).transpose(0, 2, 1, 3).reshape(RELS * HEADS, TOKENS, TW)
    stud_heads = student.reshape(RELS, TOKENS, HEADS, SW).transpose(0, 2, 1, 3).reshape(RELS * HEADS, TOKENS, SW)

    def single(stacked):
        return relation_pair(stacked[0], stacked[1], weights)
    totals, gradient = lax.map(single, (teach_heads, stud_heads))
    mean_loss = jnp.sum(totals) / (RELS * HEADS * TOKENS)
    student_grad = gradient.reshape(RELS, HEADS, TOKENS, SW).transpose(0, 2, 1, 3).reshape(RELS, TOKENS, HEADS * SW)
    return (mean_loss, student_grad)
```

```python
import functools
import math

import jax
import jax.numpy as jnp
from jax import lax
from jax.experimental import pallas as pl
from jax.experimental.pallas import tpu as pltpu
from jax.sharding import Mesh
from jax.sharding import PartitionSpec as P

TW = 256
SW = 112
HEADS = 16
SEQ = ("yl", "z", "c")
HEAD = ("yh", "x")
LOG2E = math.log2(math.e)
CT = LOG2E / math.sqrt(TW)
CS = LOG2E / math.sqrt(SW)
TOK = 256
PACK = 384
F32 = jnp.float32
BF16 = jnp.bfloat16
NT = (((1,), (1,)), ((), ()))
VMEM_LIMIT = 48 * 1024 * 1024


def whole(n):
    return [pl.BlockSpec(memory_space=pltpu.VMEM)] * n


def nt_dot(a, b):
    return lax.dot_general(a, b, NT, preferred_element_type=F32)


def prep_kernel(yl_ref, teach_ref, stud_ref, weight_ref, own_ref, give_ref):
    yl = yl_ref[0]
    weight = weight_ref[...]
    high = weight.astype(BF16).astype(F32)
    middle = (weight - high).astype(BF16).astype(F32)
    low = weight - high - middle
    row = lax.broadcasted_iota(jnp.int32, (16, TOK), 0)
    extra = jnp.where(row == 0, high, jnp.where(row == 1, middle, jnp.where(row == 2, low, 0.0)))
    packs = []
    for h in range(2):
        stud = stud_ref[h * SW : (h + 1) * SW, :].astype(F32)
        packs.append(jnp.concatenate([stud, extra], axis=0))
    first = yl == 0
    for ref, flip in ((own_ref, first), (give_ref, jnp.logical_not(first))):
        ref[:, TW:] = jnp.where(flip, packs[0], packs[1]).T.astype(BF16)
        ref[:, :TW] = jnp.where(flip, teach_ref[:, :TW].astype(F32), teach_ref[:, TW:].astype(F32)).astype(BF16)


def prepare(yl, teacher, stud_t, weights):
    packet = jax.ShapeDtypeStruct((TOK, PACK), BF16)
    return pl.pallas_call(
        prep_kernel,
        out_shape=(packet, packet),
        in_specs=[pl.BlockSpec(memory_space=pltpu.SMEM)] + whole(3),
        out_specs=tuple(whole(2)),
        name="prepare",
    )(yl, teacher, stud_t, weights)


def stud_query(ref):
    lane = lax.broadcasted_iota(jnp.int32, (TOK, PACK - TW), 1)
    return jnp.where(lane < SW, ref[:, TW:].astype(F32), 0.0).astype(BF16)


def stats_kernel(n_keys, first, last, *refs):
    queries, keys = refs[:4], refs[4 : 4 + n_keys]
    before = None if first else refs[4 + n_keys]
    out = refs[-1]
    for i, query in enumerate(queries):
        at = slice(i * TOK, (i + 1) * TOK)
        qt, qs = query[:, :TW], stud_query(query)
        state = None if first else [before[8 * k : 8 * k + 8, at] for k in range(5)]
        for key in keys:
            t = nt_dot(key[:, :TW], qt).reshape(TOK // 8, 8, TOK) * CT
            s = nt_dot(key[:, TW:], qs).reshape(TOK // 8, 8, TOK) * CS
            t_max, s_max = jnp.max(t, axis=0), jnp.max(s, axis=0)
            if state is not None:
                t_max, s_max = jnp.maximum(t_max, state[0]), jnp.maximum(s_max, state[3])
            t_exp = jnp.exp2(t - t_max[None])
            s_exp = jnp.exp2(s - s_max[None])
            t_sum, s_sum = jnp.sum(t_exp, axis=0), jnp.sum(s_exp, axis=0)
            cross = jnp.sum(t_exp * (t - s), axis=0)
            if state is not None:
                t_keep, s_keep = jnp.exp2(state[0] - t_max), jnp.exp2(state[3] - s_max)
                t_sum = t_sum + state[1] * t_keep
                cross = cross + state[2] * t_keep
                s_sum = s_sum + state[4] * s_keep
            state = [t_max, t_sum, cross, s_max, s_sum]
        if last:
            t_max, t_sum, cross, s_max, s_sum = state
            t_top = jnp.max(t_max, axis=0, keepdims=True)
            s_top = jnp.max(s_max, axis=0, keepdims=True)
            t_keep, s_keep = jnp.exp2(t_max - t_top), jnp.exp2(s_max - s_top)
            out[0:1, at] = t_top
            out[1:2, at] = jnp.sum(t_sum * t_keep, axis=0, keepdims=True)
            out[2:3, at] = jnp.sum(cross * t_keep, axis=0, keepdims=True)
            out[3:4, at] = s_top
            out[4:5, at] = jnp.sum(s_sum * s_keep, axis=0, keepdims=True)
        else:
            for k in range(5):
                out[8 * k : 8 * k + 8, at] = state[k]


def row_stats(queries, keys, before, last):
    n = len(keys)
    first = before is None
    pairs = 4 * TOK * n * TOK
    return pl.pallas_call(
        functools.partial(stats_kernel, n, first, last),
        out_shape=jax.ShapeDtypeStruct((8 if last else 40, 4 * TOK), F32),
        in_specs=whole(4 + n + (0 if first else 1)),
        out_specs=pl.BlockSpec(memory_space=pltpu.VMEM),
        compiler_params=pltpu.CompilerParams(vmem_limit_bytes=VMEM_LIMIT),
        cost_estimate=pl.CostEstimate(flops=2 * pairs * 512, bytes_accessed=pairs * 2, transcendentals=2 * pairs),
        name="row_stats",
    )(*queries, *keys, *(() if first else (before,)))


def merge_kernel(qa, qa2, qb, qb2, mine_ref, sib_ref, norm_ref, send_ref):
    total = jnp.zeros((1, TOK), F32)
    norms = []
    for i, query in enumerate((qa, qa2, qb, qb2)):
        at = slice(i * TOK, (i + 1) * TOK)
        other = slice((i ^ 1) * TOK, (i ^ 1) * TOK + TOK)
        columns = query[:, TW:].astype(F32).T
        weight = columns[SW : SW + 1] + columns[SW + 1 : SW + 2] + columns[SW + 2 : SW + 3]
        a = [mine_ref[k : k + 1, at] for k in range(5)]
        b = [sib_ref[k : k + 1, other] for k in range(5)]
        t_max, s_max = jnp.maximum(a[0], b[0]), jnp.maximum(a[3], b[3])
        ta, tb = jnp.exp2(a[0] - t_max), jnp.exp2(b[0] - t_max)
        sa, sb = jnp.exp2(a[3] - s_max), jnp.exp2(b[3] - s_max)
        t_sum, s_sum = a[1] * ta + b[1] * tb, a[4] * sa + b[4] * sb
        cross = a[2] * ta + b[2] * tb
        t_norm = t_max + jnp.log(t_sum) * LOG2E
        s_norm = s_max + jnp.log(s_sum) * LOG2E
        total = total + weight * (cross / t_sum - t_norm + s_norm)
        log_w = jnp.log(weight) * LOG2E
        norms.append((t_norm - log_w, s_norm - log_w))
        norm_ref[0:1, at] = norms[-1][0]
        norm_ref[1:2, at] = norms[-1][1]
    loss = jnp.sum(total, axis=1, keepdims=True)
    for i, k in enumerate((0, 2)):
        at = slice(i * TOK, (i + 1) * TOK)
        row = lax.broadcasted_iota(jnp.int32, (8, TOK), 0)
        block = jnp.where(row == 0, norms[k][0], jnp.where(row == 1, norms[k][1], loss))
        for z in range(8):
            send_ref[z, :, at] = block


def merge(queries, mine, sib):
    return pl.pallas_call(
        merge_kernel,
        out_shape=(jax.ShapeDtypeStruct((8, 4 * TOK), F32), jax.ShapeDtypeStruct((8, 8, 2 * TOK), F32)),
        in_specs=whole(6),
        out_specs=tuple(whole(2)),
        name="merge",
    )(*queries, mine, sib)


def fetch(keys, held, sems):
    copies = []
    for slot in range(8):
        for half in range(2):
            copy = pltpu.make_async_copy(keys[2 * slot + half], held.at[slot, half], sems.at[slot, half])
            copy.start()
            copies.append(copy)
    return copies


def column_of(row):
    return jnp.broadcast_to(row, (128, 128)).T


def row_kernel(*refs):
    queries, keys = refs[:4], refs[4:20]
    norm_ref, out, held, t_norm, s_norm, qs, sems = refs[20:]
    copies = fetch(keys, held, sems)
    for b in range(8):
        at = slice(b * 128, (b + 1) * 128)
        t_norm[at, :] = column_of(norm_ref[0:1, at])
        s_norm[at, :] = column_of(norm_ref[1:2, at])
    for i in range(4):
        qs[i] = stud_query(queries[i])
    out[...] = jnp.zeros_like(out)
    for copy in copies:
        copy.wait()

    def step(slot, carry):
        for half in range(2):
            key = held[slot, half]
            for i in range(4):
                at = slice(i * TOK, (i + 1) * TOK)
                t = nt_dot(queries[i][:, :TW], key[:, :TW]) * CT
                s = nt_dot(qs[i], key[:, TW:]) * CS
                tn, sn = t_norm[at, :], s_norm[at, :]
                p = jnp.concatenate(
                    [
                        jnp.exp2(s[:, k : k + 128] - sn) - jnp.exp2(t[:, k : k + 128] - tn)
                        for k in (0, 128)
                    ],
                    axis=1,
                ).astype(BF16)
                out[at, :] += jnp.dot(p, key[:, TW:], preferred_element_type=F32)
        return carry

    lax.fori_loop(0, 8, step, 0)


HELD = [pltpu.VMEM((8, 2, TOK, PACK), BF16)]


def row_part(queries, keys, norms):
    pairs = 4 * TOK * 4096
    return pl.pallas_call(
        row_kernel,
        out_shape=jax.ShapeDtypeStruct((4 * TOK, 128), F32),
        in_specs=whole(4) + [pl.BlockSpec(memory_space=pl.ANY)] * 16 + whole(1),
        out_specs=pl.BlockSpec(memory_space=pltpu.VMEM),
        scratch_shapes=HELD
        + [
            pltpu.VMEM((4 * TOK, 128), F32),
            pltpu.VMEM((4 * TOK, 128), F32),
            pltpu.VMEM((4, TOK, 128), BF16),
            pltpu.SemaphoreType.DMA((8, 2)),
        ],
        compiler_params=pltpu.CompilerParams(vmem_limit_bytes=VMEM_LIMIT),
        cost_estimate=pl.CostEstimate(flops=2 * pairs * 640, bytes_accessed=pairs * 4, transcendentals=2 * pairs),
        name="row_part",
    )(*queries, *keys, norms)


def col_kernel(row_at, *refs):
    z_ref, queries, keys = refs[0], refs[1:3], refs[3:19]
    stat_ref, row_ref, out0, out1, held, acc, qs, sems = refs[19:]
    copies = fetch(keys, held, sems)
    for i in range(2):
        qs[i] = stud_query(queries[i])
    acc[...] = row_ref[row_at : row_at + 2 * TOK, :]
    for copy in copies:
        copy.wait()
    here = z_ref[0]

    def step(slot, carry):
        up = (slot + 1) // 2
        offset = jnp.where(slot == 7, 4, jnp.where(slot % 2 == 1, 8 - up, up))
        source = lax.rem(here + offset, 8)
        stats = stat_ref[source]
        for half in range(2):
            key = held[slot, half]
            t_norm = stats[0:1, half * TOK : (half + 1) * TOK]
            s_norm = stats[1:2, half * TOK : (half + 1) * TOK]
            for i in range(2):
                at = slice(i * TOK, (i + 1) * TOK)
                t = nt_dot(queries[i][:, :TW], key[:, :TW]) * CT
                s = nt_dot(qs[i], key[:, TW:]) * CS
                p = (jnp.exp2(s - s_norm) - jnp.exp2(t - t_norm)).astype(BF16)
                acc[at, :] += jnp.dot(p, key[:, TW:], preferred_element_type=F32)
        return carry

    lax.fori_loop(0, 8, step, 0)
    for i, out in enumerate((out0, out1)):
        out[...] = acc[i * TOK : (i + 1) * TOK, :].T[:SW, :] * (1.0 / math.sqrt(SW))


def col_part(z, queries, keys, stats, rows, row_at):
    pairs = 2 * TOK * 4096
    part = jax.ShapeDtypeStruct((SW, TOK), F32)
    return pl.pallas_call(
        functools.partial(col_kernel, row_at),
        out_shape=(part, part),
        in_specs=[pl.BlockSpec(memory_space=pltpu.SMEM)]
        + whole(2)
        + [pl.BlockSpec(memory_space=pl.ANY)] * 16
        + whole(2),
        out_specs=tuple(whole(2)),
        scratch_shapes=HELD
        + [
            pltpu.VMEM((2 * TOK, 128), F32),
            pltpu.VMEM((2, TOK, 128), BF16),
            pltpu.SemaphoreType.DMA((8, 2)),
        ],
        compiler_params=pltpu.CompilerParams(vmem_limit_bytes=VMEM_LIMIT),
        cost_estimate=pl.CostEstimate(flops=2 * pairs * 640, bytes_accessed=pairs * 4, transcendentals=2 * pairs),
        name="col_part",
    )(z, *queries, *keys, stats, rows)


def shift(array, k):
    return lax.ppermute(array, "z", [(i, (i + k) % 8) for i in range(8)])


def swap(array, axis):
    n = 4 if isinstance(axis, tuple) else 2
    return lax.ppermute(array, axis, [(i, n - 1 - i) for i in range(n)])


def local(teacher, student, weights):
    yl, z = lax.axis_index("yl"), lax.axis_index("z")
    own, give = prepare(yl.reshape(1), teacher[0], student[0].T, weights.reshape(1, TOK))
    got = swap(give, "yl")
    queries = (own, swap(own, "c"), got, swap(got, "c"))
    right = [own, got]
    left = [own, got]
    keys = [own, got]
    state = None
    groups = [[own, got]]
    for step in range(1, 4):
        right = [shift(right[0], 1), shift(right[1], 1)]
        left = [shift(left[0], -1), shift(left[1], -1)]
        groups.append([*right, *left])
    groups.append([shift(right[0], 1), shift(left[1], -1)])
    state = None
    for g, group in enumerate(groups):
        state = row_stats(queries, group, state, g == 4)
    keys = [k for group in groups for k in group]
    norms, send = merge(queries, state, swap(state, "c"))
    stats = lax.all_to_all(send, "z", 0, 0, tiled=True)
    rows = row_part(queries, keys, norms)
    chip_loss = jnp.sum(stats[:, 2, :128], axis=0)
    losses = lax.all_to_all(jnp.broadcast_to(chip_loss[None, None], (16, 1, 128)), ("yl", *HEAD), 0, 0, tiled=True)
    here = z.reshape(1)
    b0, b1 = col_part(here, queries[2:], keys, stats, rows, 2 * TOK)
    other = swap(b0, "yl") + swap(b1, ("yl", "c"))
    a0, a1 = col_part(here, queries[:2], keys, stats, rows, 0)
    mine = a0 + swap(a1, "c")
    grad = jnp.where(yl == 0, jnp.concatenate([mine, other]), jnp.concatenate([other, mine]))
    mean_loss = jnp.sum(losses[:, 0, 0]) * (math.log(2.0) / (HEADS * 8192))
    return mean_loss, grad.T[None]


def solution(mesh):
    finer = Mesh(mesh.devices.reshape(2, 8, 2, 2, 4), ("yl", "z", "c", "yh", "x"))
    return jax.shard_map(
        local,
        mesh=finer,
        in_specs=(P(None, SEQ, HEAD), P(None, SEQ, HEAD), P(SEQ)),
        out_specs=(P(), P(None, SEQ, HEAD)),
        check_vma=False,
    )
```

```python
import functools
import math

import jax
import jax.numpy as jnp
from jax import lax
from jax.experimental import pallas as pl
from jax.experimental.pallas import tpu as pltpu
from jax.sharding import Mesh
from jax.sharding import PartitionSpec as P

TW = 256
SW = 112
HEADS = 16
SEQ = ("yl", "z", "c")
HEAD = ("yh", "x")
LOG2E = math.log2(math.e)
CT = LOG2E / math.sqrt(TW)
CS = LOG2E / math.sqrt(SW)
TOK = 256
PACK = 384
F32 = jnp.float32
BF16 = jnp.bfloat16
NT = (((1,), (1,)), ((), ()))
PARAMS = pltpu.CompilerParams(vmem_limit_bytes=20 * 1024 * 1024)


def whole(n):
    return [pl.BlockSpec(memory_space=pltpu.VMEM)] * n


HBM = pl.BlockSpec(memory_space=pltpu.HBM)
SCALAR = pl.BlockSpec(memory_space=pltpu.SMEM)
TEACH, STUD = slice(0, TW), slice(TW, PACK)


def in_hbm(array):
    return pltpu.with_memory_space_constraint(array, pltpu.HBM)


def nt_dot(a, b):
    return lax.dot_general(a, b, NT, preferred_element_type=F32)


def prep_kernel(yl_ref, teach_in, stud_in, weight_in, own_ref, give_ref, teach_ref, stud_ref, weight_ref, sems):
    copies = [
        pltpu.make_async_copy(source, target, sems.at[i])
        for i, (source, target) in enumerate(
            ((teach_in, teach_ref), (stud_in, stud_ref), (weight_in, weight_ref))
        )
    ]
    for copy in copies:
        copy.start()
    for copy in copies:
        copy.wait()
    yl = yl_ref[0]
    weight = weight_ref[...]
    high = weight.astype(BF16).astype(F32)
    middle = (weight - high).astype(BF16).astype(F32)
    low = weight - high - middle
    row = lax.broadcasted_iota(jnp.int32, (16, TOK), 0)
    extra = jnp.where(row == 0, high, jnp.where(row == 1, middle, jnp.where(row == 2, low, 0.0)))
    packs = []
    for h in range(2):
        stud = stud_ref[h * SW : (h + 1) * SW, :].astype(F32)
        packs.append(jnp.concatenate([stud, extra], axis=0))
    first = yl == 0
    for ref, flip in ((own_ref, first), (give_ref, jnp.logical_not(first))):
        ref[:, TW:] = jnp.where(flip, packs[0], packs[1]).T.astype(BF16)
        ref[:, :TW] = jnp.where(flip, teach_ref[:, :TW].astype(F32), teach_ref[:, TW:].astype(F32)).astype(BF16)


def prepare(yl, teacher, stud_t, weights):
    packet = jax.ShapeDtypeStruct((TOK, PACK), BF16)
    return pl.pallas_call(
        prep_kernel,
        out_shape=(packet, packet),
        in_specs=[SCALAR] + [HBM] * 3,
        out_specs=tuple(whole(2)),
        scratch_shapes=[
            pltpu.VMEM((TOK, 2 * TW), BF16),
            pltpu.VMEM((2 * SW, TOK), BF16),
            pltpu.VMEM((1, TOK), F32),
            pltpu.SemaphoreType.DMA((3,)),
        ],
        compiler_params=PARAMS,
        name="prepare",
    )(yl, in_hbm(teacher), in_hbm(stud_t), in_hbm(weights))


def pair_kernel(own, sib, out):
    out[:TOK, :] = own[...]
    out[TOK:, :] = sib[...]


def pair_up(own, sib):
    return pl.pallas_call(
        pair_kernel,
        out_shape=jax.ShapeDtypeStruct((2 * TOK, PACK), BF16),
        in_specs=whole(2),
        out_specs=whole(1)[0],
        compiler_params=PARAMS,
        name="pair_up",
    )(own, sib)


def open_packets(pairs, held, weight_ref):
    lane = lax.broadcasted_iota(jnp.int32, (2 * TOK, PACK - TW), 1)
    for i, pair in enumerate(pairs):
        at = slice(2 * i * TOK, 2 * (i + 1) * TOK)
        held[at, :TW] = pair[:, :TW]
        stud = pair[:, TW:].astype(F32)
        held[at, TW:] = jnp.where(lane < SW, stud, 0.0).astype(BF16)
        columns = stud.T
        weight = columns[SW : SW + 1] + columns[SW + 1 : SW + 2] + columns[SW + 2 : SW + 3]
        weight_ref[0:1, at] = weight
        weight_ref[1:2, at] = jnp.log(weight) * LOG2E


def take_stats(held, key, before, out, last):
    for i in range(2):
        at = slice(2 * i * TOK, 2 * (i + 1) * TOK)
        t = nt_dot(key[:, TEACH], held[at, TEACH]).reshape(TOK // 4, 8, 2 * TOK) * CT
        s = nt_dot(key[:, STUD], held[at, STUD]).reshape(TOK // 4, 8, 2 * TOK) * CS
        t_max, s_max = jnp.max(t, axis=0), jnp.max(s, axis=0)
        if before is not None:
            state = [before[8 * k : 8 * k + 8, at] for k in range(5)]
            t_max, s_max = jnp.maximum(t_max, state[0]), jnp.maximum(s_max, state[3])
        t_exp = jnp.exp2(t - t_max[None])
        s_exp = jnp.exp2(s - s_max[None])
        t_sum, s_sum = jnp.sum(t_exp, axis=0), jnp.sum(s_exp, axis=0)
        cross = jnp.sum(t_exp * (t - s), axis=0)
        if before is not None:
            t_keep, s_keep = jnp.exp2(state[0] - t_max), jnp.exp2(state[3] - s_max)
            t_sum = t_sum + state[1] * t_keep
            cross = cross + state[2] * t_keep
            s_sum = s_sum + state[4] * s_keep
        if last:
            t_top = jnp.max(t_max, axis=0, keepdims=True)
            s_top = jnp.max(s_max, axis=0, keepdims=True)
            t_keep, s_keep = jnp.exp2(t_max - t_top), jnp.exp2(s_max - s_top)
            out[0:1, at] = t_top
            out[1:2, at] = jnp.sum(t_sum * t_keep, axis=0, keepdims=True)
            out[2:3, at] = jnp.sum(cross * t_keep, axis=0, keepdims=True)
            out[3:4, at] = s_top
            out[4:5, at] = jnp.sum(s_sum * s_keep, axis=0, keepdims=True)
        else:
            for k, value in enumerate((t_max, t_sum, cross, s_max, s_sum)):
                out[8 * k : 8 * k + 8, at] = value


def own_keys(held, columns):
    return jnp.concatenate([held[:TOK, columns], held[2 * TOK : 3 * TOK, columns]], axis=0)


def first_kernel(own_ref, got_ref, state, held, weight_ref):
    open_packets((own_ref, got_ref), held, weight_ref)
    take_stats(held, own_keys(held, slice(None)), None, state, False)


def more_kernel(fetched, last, held, *refs):
    n = len(refs) - (4 if fetched else 2)
    before, out = refs[n : n + 2]
    if fetched:
        key, sem = refs[n + 2 :]
        copy = pltpu.make_async_copy(refs[0], key, sem.at[0])
        copy.start()
        copy.wait()
    else:
        key = refs[0] if n == 1 else jnp.concatenate([refs[0][...], refs[1][...]], axis=0)
    take_stats(held, key, before, out, last)


STAT_PAIRS = 4 * TOK * 2 * TOK
STAT_COST = pl.CostEstimate(flops=2 * STAT_PAIRS * 512, bytes_accessed=STAT_PAIRS * 4, transcendentals=2 * STAT_PAIRS)


def first_stats(own_pair, got_pair):
    return pl.pallas_call(
        first_kernel,
        out_shape=(
            jax.ShapeDtypeStruct((40, 4 * TOK), F32),
            jax.ShapeDtypeStruct((4 * TOK, PACK), BF16),
            jax.ShapeDtypeStruct((8, 4 * TOK), F32),
        ),
        in_specs=whole(2),
        out_specs=tuple(whole(3)),
        compiler_params=PARAMS,
        cost_estimate=STAT_COST,
        name="first_stats",
    )(own_pair, got_pair)


def more_stats(held, keys, before, last=False, fetched=False):
    return pl.pallas_call(
        functools.partial(more_kernel, fetched, last),
        out_shape=jax.ShapeDtypeStruct((8 if last else 40, 4 * TOK), F32),
        in_specs=whole(1) + ([HBM] if fetched else whole(len(keys))) + whole(1),
        out_specs=whole(1)[0],
        scratch_shapes=[pltpu.VMEM((2 * TOK, PACK), BF16), pltpu.SemaphoreType.DMA((1,))] if fetched else [],
        compiler_params=PARAMS,
        cost_estimate=STAT_COST,
        name="more_stats",
    )(held, *((in_hbm(k) for k in keys) if fetched else keys), before)


def merge_kernel(mine, sib, weight_ref, norm_ref, send_ref):
    total = jnp.zeros((1, TOK), F32)
    for i in range(4):
        at = slice(i * TOK, (i + 1) * TOK)
        there = slice((i ^ 1) * TOK, ((i ^ 1) + 1) * TOK)
        a = [mine[k : k + 1, at] for k in range(5)]
        b = [sib[k : k + 1, there] for k in range(5)]
        t_max, s_max = jnp.maximum(a[0], b[0]), jnp.maximum(a[3], b[3])
        ta, tb = jnp.exp2(a[0] - t_max), jnp.exp2(b[0] - t_max)
        sa, sb = jnp.exp2(a[3] - s_max), jnp.exp2(b[3] - s_max)
        t_sum, s_sum = a[1] * ta + b[1] * tb, a[4] * sa + b[4] * sb
        cross = a[2] * ta + b[2] * tb
        t_norm = t_max + jnp.log(t_sum) * LOG2E
        s_norm = s_max + jnp.log(s_sum) * LOG2E
        total = total + weight_ref[0:1, at] * (cross / t_sum - t_norm + s_norm)
        t_norm, s_norm = t_norm - weight_ref[1:2, at], s_norm - weight_ref[1:2, at]
        norm_ref[0:1, at] = t_norm
        norm_ref[1:2, at] = s_norm
        for z in range(8):
            send_ref[z, 0:1, at] = t_norm
            send_ref[z, 1:2, at] = s_norm
    loss = jnp.broadcast_to(jnp.sum(total, axis=1, keepdims=True), (2, 128))
    for z in range(8):
        send_ref[z, :, 4 * TOK :] = loss


def merge(mine, sib, weight):
    return pl.pallas_call(
        merge_kernel,
        out_shape=(jax.ShapeDtypeStruct((8, 4 * TOK), F32), jax.ShapeDtypeStruct((8, 2, 4 * TOK + 128), F32)),
        in_specs=whole(3),
        out_specs=tuple(whole(2)),
        compiler_params=PARAMS,
        name="merge",
    )(mine, sib, weight)


def column_of(row):
    return jnp.broadcast_to(row, (128, 128)).T


def slopes_of(t, s, t_norm, s_norm):
    return jnp.exp2(s - s_norm) - jnp.exp2(t - t_norm)


class Keys:
    def __init__(self, held, refs, late, sems):
        self.held, self.near, self.far, self.opposite, self.late = held, refs[:4], refs[4:6], refs[6:8], late
        self.copies = [pltpu.make_async_copy(self.far[i], late.at[i], sems.at[i]) for i in range(2)]
        for copy in self.copies:
            copy.start()

    def wait(self):
        for copy in self.copies:
            copy.wait()

    def block(self, slot, columns):
        if slot == 0:
            return own_keys(self.held, columns)
        if slot <= 4:
            return self.near[slot - 1][:, columns]
        if slot <= 6:
            return self.late[slot - 5, :, columns]
        return jnp.concatenate([self.opposite[0][:, columns], self.opposite[1][:, columns]], axis=0)


KEY_SPECS = whole(4) + [HBM] * 2 + whole(2)
KEY_SCRATCH = [pltpu.VMEM((2, 2 * TOK, PACK), BF16), pltpu.SemaphoreType.DMA((3,))]


def as_operands(packets):
    return [*packets[:4], *(in_hbm(p) for p in packets[4:6]), *packets[6:]]


def row_kernel(held, norm_ref, *refs):
    result, t_norm, s_norm, out, late, sems = refs[8:]
    keys = Keys(held, refs[:8], late, sems)
    for b in range(8):
        at = slice(b * 128, (b + 1) * 128)
        t_norm[at, :] = column_of(norm_ref[0:1, at])
        s_norm[at, :] = column_of(norm_ref[1:2, at])
    keys.wait()

    def step(half, carry):
        at = pl.ds(pl.multiple_of(half * 2 * TOK, 2 * TOK), 2 * TOK)
        tn, sn = t_norm[at, :], s_norm[at, :]
        for slot in range(8):
            stud = keys.block(slot, STUD)
            t = nt_dot(held[at, TEACH], keys.block(slot, TEACH)) * CT
            s = nt_dot(held[at, STUD], stud) * CS
            p = jnp.concatenate(
                [slopes_of(t[:, k : k + 128], s[:, k : k + 128], tn, sn) for k in range(0, 2 * TOK, 128)], axis=1
            )
            part = jnp.dot(p.astype(BF16), stud, preferred_element_type=F32)
            out[at, :] = part if slot == 0 else out[at, :] + part
        copy = pltpu.make_async_copy(out.at[at, :], result.at[at, :], sems.at[2])
        copy.start()
        copy.wait()
        return carry

    lax.fori_loop(0, 2, step, 0)


def row_part(held, norms, packets):
    pairs = 4 * TOK * 4096
    return pl.pallas_call(
        row_kernel,
        out_shape=pltpu.HBM((4 * TOK, 128), F32),
        in_specs=whole(2) + KEY_SPECS,
        out_specs=HBM,
        scratch_shapes=[pltpu.VMEM((4 * TOK, 128), F32)] * 3 + KEY_SCRATCH,
        compiler_params=PARAMS,
        cost_estimate=pl.CostEstimate(flops=2 * pairs * 640, bytes_accessed=pairs * 4, transcendentals=2 * pairs),
        name="row_part",
    )(held, norms, *as_operands(packets))


def col_kernel(query_at, place_ref, held, stat_ref, *refs):
    row_ref, keep, give, acc, rows, late, sems = refs[8:]
    keys = Keys(held, refs[:8], late, sems)
    at = slice(query_at, query_at + 2 * TOK)
    copy = pltpu.make_async_copy(row_ref.at[at, :], rows, sems.at[2])
    copy.start()
    toward = jnp.where(place_ref[0] == 0, 7, 1)
    for slot in range(8):
        if slot == 5:
            keys.wait()
        stats = stat_ref[lax.rem(place_ref[1] + toward * ((slot + 1) // 2), 8)]
        if slot in (0, 7):
            stats = jnp.concatenate([stats[:, :TOK], stats[:, 2 * TOK : 3 * TOK]], axis=1)
        else:
            plane = 2 * TOK * ((slot - 1) % 2)
            stats = stats[:, plane : plane + 2 * TOK]
        stud = keys.block(slot, STUD)
        t = nt_dot(held[at, TEACH], keys.block(slot, TEACH)) * CT
        s = nt_dot(held[at, STUD], stud) * CS
        p = slopes_of(t, s, stats[0:1], stats[1:2]).astype(BF16)
        part = jnp.dot(p, stud, preferred_element_type=F32)
        acc[...] = part if slot == 0 else acc[...] + part
    copy.wait()
    for i, out in enumerate((keep, give)):
        part = slice(i * TOK, (i + 1) * TOK)
        out[...] = (acc[part, :] + rows[part, :]).T[:SW, :] * (1.0 / math.sqrt(SW))


def col_part(place, held, stats, packets, rows, query_at):
    pairs = 2 * TOK * 4096
    part = jax.ShapeDtypeStruct((SW, TOK), F32)
    return pl.pallas_call(
        functools.partial(col_kernel, query_at),
        out_shape=(part, part),
        in_specs=[SCALAR] + whole(2) + KEY_SPECS + [HBM],
        out_specs=tuple(whole(2)),
        scratch_shapes=[pltpu.VMEM((2 * TOK, 128), F32)] * 2 + KEY_SCRATCH,
        compiler_params=PARAMS,
        cost_estimate=pl.CostEstimate(flops=2 * pairs * 640, bytes_accessed=pairs * 4, transcendentals=2 * pairs),
        name="col_part",
    )(place, held, stats, *as_operands(packets), in_hbm(rows))


def onward(array):
    pairs = [(2 * z + c, 2 * ((z + (-1) ** c) % 8) + c) for z in range(8) for c in range(2)]
    return lax.ppermute(array, ("z", "c"), pairs)


def tied(*arrays):
    return lax.optimization_barrier(arrays)


def swap(array, axis):
    n = 4 if isinstance(axis, tuple) else 2
    return lax.ppermute(array, axis, [(i, n - 1 - i) for i in range(n)])


def local(teacher, student, weights):
    yl, z, c = lax.axis_index("yl"), lax.axis_index("z"), lax.axis_index("c")
    own, give = prepare(yl.reshape(1), teacher[0], student[0].T, weights.reshape(1, TOK))
    got = swap(give, "yl")
    own_pair = pair_up(own, swap(own, "c"))
    a1 = onward(own_pair)
    got_pair = pair_up(got, swap(got, "c"))
    a1, sent_pair = tied(a1, got_pair)
    b1 = onward(sent_pair)
    a2 = onward(a1)
    state, held, weight = first_stats(own_pair, got_pair)
    b1, state = tied(b1, state)
    b2 = onward(b1)
    state = more_stats(held, (a1,), state)
    a2, state = tied(a2, state)
    a3 = onward(a2)
    state = more_stats(held, (b1,), state)
    b2, state = tied(b2, state)
    b3 = onward(b2)
    state = more_stats(held, (a2,), state)
    a3, state = tied(a3, state)
    a4 = onward(a3[:TOK])
    state = more_stats(held, (b2,), state)
    b3, state = tied(b3, state)
    b4 = onward(b3[:TOK])
    for far in (a3, b3):
        state = more_stats(held, (far,), state, fetched=True)
    state = more_stats(held, (a4, b4), state, last=True)
    packets = (a1, b1, a2, b2, a3, b3, a4, b4)
    norms, send = merge(state, swap(state, "c"), weight)
    stats = lax.all_to_all(send, "z", 0, 0, tiled=True)
    rows = row_part(held, norms, packets)
    chip_loss = jnp.sum(stats[:, 0, 4 * TOK :], axis=0)
    losses = lax.all_to_all(jnp.broadcast_to(chip_loss[None, None], (16, 1, 128)), ("yl", *HEAD), 0, 0, tiled=True)
    place = jnp.stack([c, z])
    far_keep, far_give = col_part(place, held, stats, packets, rows, 2 * TOK)
    other = swap(far_keep, "yl") + swap(far_give, ("yl", "c"))
    rows, other = tied(rows, other)
    near_keep, near_give = col_part(place, held, stats, packets, rows, 0)
    mine = near_keep + swap(near_give, "c")
    grad = jnp.where(yl == 0, jnp.concatenate([mine, other]), jnp.concatenate([other, mine]))
    mean_loss = jnp.sum(losses[:, 0, 0]) * (math.log(2.0) / (HEADS * 8192))
    return mean_loss, grad.T[None]


def solution(mesh):
    finer = Mesh(mesh.devices.reshape(2, 8, 2, 2, 4), ("yl", "z", "c", "yh", "x"))
    return jax.shard_map(
        local,
        mesh=finer,
        in_specs=(P(None, SEQ, HEAD), P(None, SEQ, HEAD), P(SEQ)),
        out_specs=(P(), P(None, SEQ, HEAD)),
        check_vma=False,
    )
```

```python
import functools
import math

import jax
import jax.numpy as jnp
from jax import lax
from jax.experimental import pallas as pl
from jax.experimental.pallas import tpu as pltpu
from jax.sharding import Mesh
from jax.sharding import PartitionSpec as P

TW = 256
SW = 112
HEADS = 16
SEQ = ("yl", "z", "c")
HEAD = ("yh", "x")
LOG2E = math.log2(math.e)
CT = LOG2E / math.sqrt(TW)
CS = LOG2E / math.sqrt(SW)
TOK = 256
PACK = 384
F32 = jnp.float32
BF16 = jnp.bfloat16
NT = (((1,), (1,)), ((), ()))
PARAMS = pltpu.CompilerParams(vmem_limit_bytes=20 * 1024 * 1024)


def whole(n):
    return [pl.BlockSpec(memory_space=pltpu.VMEM)] * n


HBM = pl.BlockSpec(memory_space=pltpu.HBM)
SCALAR = pl.BlockSpec(memory_space=pltpu.SMEM)
TEACH, STUD = slice(0, TW), slice(TW, PACK)


def in_hbm(array):
    return pltpu.with_memory_space_constraint(array, pltpu.HBM)


def nt_dot(a, b):
    return lax.dot_general(a, b, NT, preferred_element_type=F32)


def prep_kernel(yl_ref, teach_in, stud_in, weight_in, own_ref, give_ref, teach_ref, stud_ref, weight_ref, sems):
    copies = [
        pltpu.make_async_copy(source, target, sems.at[i])
        for i, (source, target) in enumerate(
            ((teach_in, teach_ref), (stud_in, stud_ref), (weight_in, weight_ref))
        )
    ]
    for copy in copies:
        copy.start()
    for copy in copies:
        copy.wait()
    yl = yl_ref[0]
    weight = weight_ref[...]
    high = weight.astype(BF16).astype(F32)
    middle = (weight - high).astype(BF16).astype(F32)
    low = weight - high - middle
    row = lax.broadcasted_iota(jnp.int32, (16, TOK), 0)
    extra = jnp.where(row == 0, high, jnp.where(row == 1, middle, jnp.where(row == 2, low, 0.0)))
    packs = []
    for h in range(2):
        stud = stud_ref[h * SW : (h + 1) * SW, :].astype(F32)
        packs.append(jnp.concatenate([stud, extra], axis=0))
    first = yl == 0
    for ref, flip in ((own_ref, first), (give_ref, jnp.logical_not(first))):
        ref[:, TW:] = jnp.where(flip, packs[0], packs[1]).T.astype(BF16)
        ref[:, :TW] = jnp.where(flip, teach_ref[:, :TW].astype(F32), teach_ref[:, TW:].astype(F32)).astype(BF16)


def prepare(yl, teacher, stud_t, weights):
    packet = jax.ShapeDtypeStruct((TOK, PACK), BF16)
    return pl.pallas_call(
        prep_kernel,
        out_shape=(packet, packet),
        in_specs=[SCALAR] + [HBM] * 3,
        out_specs=tuple(whole(2)),
        scratch_shapes=[
            pltpu.VMEM((TOK, 2 * TW), BF16),
            pltpu.VMEM((2 * SW, TOK), BF16),
            pltpu.VMEM((1, TOK), F32),
            pltpu.SemaphoreType.DMA((3,)),
        ],
        compiler_params=PARAMS,
        name="prepare",
    )(yl, in_hbm(teacher), in_hbm(stud_t), in_hbm(weights))


def pair_kernel(own, sib, out):
    out[:TOK, :] = own[...]
    out[TOK:, :] = sib[...]


def pair_up(own, sib):
    return pl.pallas_call(
        pair_kernel,
        out_shape=jax.ShapeDtypeStruct((2 * TOK, PACK), BF16),
        in_specs=whole(2),
        out_specs=whole(1)[0],
        compiler_params=PARAMS,
        name="pair_up",
    )(own, sib)


def open_packets(pairs, held, weight_ref):
    lane = lax.broadcasted_iota(jnp.int32, (2 * TOK, PACK - TW), 1)
    for i, pair in enumerate(pairs):
        at = slice(2 * i * TOK, 2 * (i + 1) * TOK)
        held[at, :TW] = pair[:, :TW]
        stud = pair[:, TW:].astype(F32)
        held[at, TW:] = jnp.where(lane < SW, stud, 0.0).astype(BF16)
        columns = stud.T
        weight = columns[SW : SW + 1] + columns[SW + 1 : SW + 2] + columns[SW + 2 : SW + 3]
        weight_ref[0:1, at] = weight
        weight_ref[1:2, at] = jnp.log(weight) * LOG2E


def take_stats(held, key, before, out, last):
    for i in range(2):
        at = slice(2 * i * TOK, 2 * (i + 1) * TOK)
        t = nt_dot(key[:, TEACH], held[at, TEACH]).reshape(TOK // 4, 8, 2 * TOK) * CT
        s = nt_dot(key[:, STUD], held[at, STUD]).reshape(TOK // 4, 8, 2 * TOK) * CS
        t_max, s_max = jnp.max(t, axis=0), jnp.max(s, axis=0)
        if before is not None:
            state = [before[8 * k : 8 * k + 8, at] for k in range(5)]
            t_max, s_max = jnp.maximum(t_max, state[0]), jnp.maximum(s_max, state[3])
        t_exp = jnp.exp2(t - t_max[None])
        s_exp = jnp.exp2(s - s_max[None])
        t_sum, s_sum = jnp.sum(t_exp, axis=0), jnp.sum(s_exp, axis=0)
        cross = jnp.sum(t_exp * (t - s), axis=0)
        if before is not None:
            t_keep, s_keep = jnp.exp2(state[0] - t_max), jnp.exp2(state[3] - s_max)
            t_sum = t_sum + state[1] * t_keep
            cross = cross + state[2] * t_keep
            s_sum = s_sum + state[4] * s_keep
        if last:
            t_top = jnp.max(t_max, axis=0, keepdims=True)
            s_top = jnp.max(s_max, axis=0, keepdims=True)
            t_keep, s_keep = jnp.exp2(t_max - t_top), jnp.exp2(s_max - s_top)
            out[0:1, at] = t_top
            out[1:2, at] = jnp.sum(t_sum * t_keep, axis=0, keepdims=True)
            out[2:3, at] = jnp.sum(cross * t_keep, axis=0, keepdims=True)
            out[3:4, at] = s_top
            out[4:5, at] = jnp.sum(s_sum * s_keep, axis=0, keepdims=True)
        else:
            for k, value in enumerate((t_max, t_sum, cross, s_max, s_sum)):
                out[8 * k : 8 * k + 8, at] = value


def own_keys(held, columns):
    return jnp.concatenate([held[:TOK, columns], held[2 * TOK : 3 * TOK, columns]], axis=0)


def first_kernel(own_ref, got_ref, state, held, weight_ref):
    open_packets((own_ref, got_ref), held, weight_ref)
    take_stats(held, own_keys(held, slice(None)), None, state, False)


def more_kernel(last, held, *refs):
    *keys, before, out = refs
    key = keys[0] if len(keys) == 1 else jnp.concatenate([k[...] for k in keys], axis=0)
    take_stats(held, key, before, out, last)


STAT_PAIRS = 4 * TOK * 2 * TOK
STAT_COST = pl.CostEstimate(flops=2 * STAT_PAIRS * 512, bytes_accessed=STAT_PAIRS * 4, transcendentals=2 * STAT_PAIRS)


def first_stats(own_pair, got_pair):
    return pl.pallas_call(
        first_kernel,
        out_shape=(
            jax.ShapeDtypeStruct((40, 4 * TOK), F32),
            jax.ShapeDtypeStruct((4 * TOK, PACK), BF16),
            jax.ShapeDtypeStruct((8, 4 * TOK), F32),
        ),
        in_specs=whole(2),
        out_specs=tuple(whole(3)),
        compiler_params=PARAMS,
        cost_estimate=STAT_COST,
        name="first_stats",
    )(own_pair, got_pair)


def more_stats(held, keys, before, last=False):
    return pl.pallas_call(
        functools.partial(more_kernel, last),
        out_shape=jax.ShapeDtypeStruct((8 if last else 40, 4 * TOK), F32),
        in_specs=whole(2 + len(keys)),
        out_specs=whole(1)[0],
        input_output_aliases={} if last else {1 + len(keys): 0},
        compiler_params=PARAMS,
        cost_estimate=STAT_COST,
        name="more_stats",
    )(held, *keys, before)


def merge_kernel(mine, sib, weight_ref, norm_ref, send_ref):
    total = jnp.zeros((1, TOK), F32)
    for i in range(4):
        at = slice(i * TOK, (i + 1) * TOK)
        there = slice((i ^ 1) * TOK, ((i ^ 1) + 1) * TOK)
        a = [mine[k : k + 1, at] for k in range(5)]
        b = [sib[k : k + 1, there] for k in range(5)]
        t_max, s_max = jnp.maximum(a[0], b[0]), jnp.maximum(a[3], b[3])
        ta, tb = jnp.exp2(a[0] - t_max), jnp.exp2(b[0] - t_max)
        sa, sb = jnp.exp2(a[3] - s_max), jnp.exp2(b[3] - s_max)
        t_sum, s_sum = a[1] * ta + b[1] * tb, a[4] * sa + b[4] * sb
        cross = a[2] * ta + b[2] * tb
        t_norm = t_max + jnp.log(t_sum) * LOG2E
        s_norm = s_max + jnp.log(s_sum) * LOG2E
        total = total + weight_ref[0:1, at] * (cross / t_sum - t_norm + s_norm)
        t_norm, s_norm = t_norm - weight_ref[1:2, at], s_norm - weight_ref[1:2, at]
        norm_ref[0:1, at] = t_norm
        norm_ref[1:2, at] = s_norm
        for z in range(8):
            send_ref[z, 0:1, at] = t_norm
            send_ref[z, 1:2, at] = s_norm
    loss = jnp.broadcast_to(jnp.sum(total, axis=1, keepdims=True), (2, 128))
    for z in range(8):
        send_ref[z, :, 4 * TOK :] = loss


def merge(mine, sib, weight):
    return pl.pallas_call(
        merge_kernel,
        out_shape=(jax.ShapeDtypeStruct((8, 4 * TOK), F32), jax.ShapeDtypeStruct((8, 2, 4 * TOK + 128), F32)),
        in_specs=whole(3),
        out_specs=tuple(whole(2)),
        compiler_params=PARAMS,
        name="merge",
    )(mine, sib, weight)


def column_of(row):
    return jnp.broadcast_to(row, (128, 128)).T


def slopes_of(t, s, t_norm, s_norm):
    return jnp.exp2(s - s_norm) - jnp.exp2(t - t_norm)


class Keys:
    def __init__(self, held, refs, late, sems):
        self.held, self.near, self.opposite, self.far, self.late = held, refs[:4], refs[4:6], refs[6:8], late
        self.copies = [pltpu.make_async_copy(self.far[i], late.at[i], sems.at[i]) for i in range(2)]

    def start(self):
        for copy in self.copies:
            copy.start()

    def wait(self):
        for copy in self.copies:
            copy.wait()

    def block(self, slot, columns):
        if slot == 0:
            return own_keys(self.held, columns)
        if slot <= 4:
            return self.near[slot - 1][:, columns]
        if slot == 5:
            return jnp.concatenate([self.opposite[0][:, columns], self.opposite[1][:, columns]], axis=0)
        return self.late[slot - 6, :, columns]


STEPS = (0, 2, 2, 3, 3, 4, 1, 1)
KEY_SPECS = whole(6) + [HBM] * 2
KEY_SCRATCH = [pltpu.VMEM((2, 2 * TOK, PACK), BF16), pltpu.SemaphoreType.DMA((4,))]


def as_operands(packets):
    return [*packets[:6], *(in_hbm(p) for p in packets[6:])]


def row_kernel(held, norm_ref, *refs):
    result, t_norm, s_norm, out, late, sems = refs[8:]
    keys = Keys(held, refs[:8], late, sems)
    keys.start()
    for b in range(8):
        at = slice(b * 128, (b + 1) * 128)
        t_norm[at, :] = column_of(norm_ref[0:1, at])
        s_norm[at, :] = column_of(norm_ref[1:2, at])

    def step(half, carry):
        at = pl.ds(pl.multiple_of(half * 2 * TOK, 2 * TOK), 2 * TOK)
        tn, sn = t_norm[at, :], s_norm[at, :]
        for slot in range(8):
            if slot == 6:
                pl.when(half == 0)(keys.wait)
            stud = keys.block(slot, STUD)
            t = nt_dot(held[at, TEACH], keys.block(slot, TEACH)) * CT
            s = nt_dot(held[at, STUD], stud) * CS
            p = jnp.concatenate(
                [slopes_of(t[:, k : k + 128], s[:, k : k + 128], tn, sn) for k in range(0, 2 * TOK, 128)], axis=1
            )
            part = jnp.dot(p.astype(BF16), stud, preferred_element_type=F32)
            out[at, :] = part if slot == 0 else out[at, :] + part
        pltpu.make_async_copy(out.at[at, :], result.at[at, :], sems.at[2 + half]).start()
        return carry

    lax.fori_loop(0, 2, step, 0)
    for half in range(2):
        at = slice(half * 2 * TOK, (half + 1) * 2 * TOK)
        pltpu.make_async_copy(out.at[at, :], result.at[at, :], sems.at[2 + half]).wait()


def row_part(held, norms, packets):
    pairs = 4 * TOK * 4096
    return pl.pallas_call(
        row_kernel,
        out_shape=pltpu.HBM((4 * TOK, 128), F32),
        in_specs=whole(2) + KEY_SPECS,
        out_specs=HBM,
        scratch_shapes=[pltpu.VMEM((4 * TOK, 128), F32)] * 3 + KEY_SCRATCH,
        compiler_params=PARAMS,
        cost_estimate=pl.CostEstimate(flops=2 * pairs * 640, bytes_accessed=pairs * 4, transcendentals=2 * pairs),
        name="row_part",
    )(held, norms, *as_operands(packets))


def col_kernel(query_at, place_ref, held, stat_ref, *refs):
    row_ref, keep, give, acc, rows, late, sems = refs[8:]
    keys = Keys(held, refs[:8], late, sems)
    keys.start()
    at = slice(query_at, query_at + 2 * TOK)
    copy = pltpu.make_async_copy(row_ref.at[at, :], rows, sems.at[2])
    copy.start()
    toward = jnp.where(place_ref[0] == 0, 7, 1)
    for slot in range(8):
        if slot == 6:
            keys.wait()
            copy.wait()
        stats = stat_ref[lax.rem(place_ref[1] + toward * STEPS[slot], 8)]
        if slot in (0, 5):
            stats = jnp.concatenate([stats[:, :TOK], stats[:, 2 * TOK : 3 * TOK]], axis=1)
        else:
            plane = 2 * TOK * (1 - slot % 2 if slot < 5 else slot % 2)
            stats = stats[:, plane : plane + 2 * TOK]
        stud = keys.block(slot, STUD)
        t = nt_dot(held[at, TEACH], keys.block(slot, TEACH)) * CT
        s = nt_dot(held[at, STUD], stud) * CS
        p = slopes_of(t, s, stats[0:1], stats[1:2]).astype(BF16)
        part = jnp.dot(p, stud, preferred_element_type=F32)
        acc[...] = part if slot == 0 else acc[...] + part
    for i, out in enumerate((keep, give)):
        part = slice(i * TOK, (i + 1) * TOK)
        out[...] = (acc[part, :] + rows[part, :]).T[:SW, :] * (1.0 / math.sqrt(SW))


def col_part(place, held, stats, packets, rows, query_at):
    pairs = 2 * TOK * 4096
    part = jax.ShapeDtypeStruct((SW, TOK), F32)
    return pl.pallas_call(
        functools.partial(col_kernel, query_at),
        out_shape=(part, part),
        in_specs=[SCALAR] + whole(2) + KEY_SPECS + [HBM],
        out_specs=tuple(whole(2)),
        scratch_shapes=[pltpu.VMEM((2 * TOK, 128), F32)] * 2 + KEY_SCRATCH,
        compiler_params=PARAMS,
        cost_estimate=pl.CostEstimate(flops=2 * pairs * 640, bytes_accessed=pairs * 4, transcendentals=2 * pairs),
        name="col_part",
    )(place, held, stats, *as_operands(packets), in_hbm(rows))


def onward(array):
    pairs = [(2 * z + c, 2 * ((z + (-1) ** c) % 8) + c) for z in range(8) for c in range(2)]
    return lax.ppermute(array, ("z", "c"), pairs)


def tied(*arrays):
    return lax.optimization_barrier(arrays)


def swap(array, axis):
    n = 4 if isinstance(axis, tuple) else 2
    return lax.ppermute(array, axis, [(i, n - 1 - i) for i in range(n)])


def local(teacher, student, weights):
    yl, z, c = lax.axis_index("yl"), lax.axis_index("z"), lax.axis_index("c")
    own, give = prepare(yl.reshape(1), teacher[0], student[0].T, weights.reshape(1, TOK))
    got = swap(give, "yl")
    own_pair = pair_up(own, swap(own, "c"))
    a1 = onward(own_pair)
    got_pair = pair_up(got, swap(got, "c"))
    a1, sent_pair = tied(a1, got_pair)
    b1 = onward(sent_pair)
    a2 = onward(a1)
    state, held, weight = first_stats(own_pair, got_pair)
    b1, state = tied(b1, state)
    b2 = onward(b1)
    state = more_stats(held, (a1,), state)
    a2, state = tied(a2, state)
    a3 = onward(a2)
    state = more_stats(held, (b1,), state)
    b2, state = tied(b2, state)
    b3 = onward(b2)
    state = more_stats(held, (a2,), state)
    a3, state = tied(a3, state)
    a4 = onward(a3[:TOK])
    state = more_stats(held, (b2,), state)
    b3, state = tied(b3, state)
    b4 = onward(b3[:TOK])
    for packets in (a3, b3):
        state = more_stats(held, (packets,), state)
    state = more_stats(held, (a4, b4), state, last=True)
    packets = (a2, b2, a3, b3, a4, b4, a1, b1)
    norms, send = merge(state, swap(state, "c"), weight)
    stats = lax.all_to_all(send, "z", 0, 0, tiled=True)
    rows = row_part(held, norms, packets)
    chip_loss = jnp.sum(stats[:, 0, 4 * TOK :], axis=0)
    losses = lax.all_to_all(jnp.broadcast_to(chip_loss[None, None], (16, 1, 128)), ("yl", *HEAD), 0, 0, tiled=True)
    place = jnp.stack([c, z])
    far_keep, far_give = col_part(place, held, stats, packets, rows, 2 * TOK)
    other = swap(far_keep, "yl") + swap(far_give, ("yl", "c"))
    rows, other = tied(rows, other)
    near_keep, near_give = col_part(place, held, stats, packets, rows, 0)
    mine = near_keep + swap(near_give, "c")
    grad = jnp.where(yl == 0, jnp.concatenate([mine, other]), jnp.concatenate([other, mine]))
    mean_loss = jnp.sum(losses[:, 0, 0]) * (math.log(2.0) / (HEADS * 8192))
    return mean_loss, grad.T[None]


def solution(mesh):
    finer = Mesh(mesh.devices.reshape(2, 8, 2, 2, 4), ("yl", "z", "c", "yh", "x"))
    return jax.shard_map(
        local,
        mesh=finer,
        in_specs=(P(None, SEQ, HEAD), P(None, SEQ, HEAD), P(SEQ)),
        out_specs=(P(), P(None, SEQ, HEAD)),
        check_vma=False,
    )
```

```python
import functools
import math

import jax
import jax.numpy as jnp
from jax import lax
from jax.experimental import pallas as pl
from jax.experimental.pallas import tpu as pltpu
from jax.sharding import Mesh
from jax.sharding import PartitionSpec as P

TW = 256
SW = 112
HEADS = 16
SEQ = ("yl", "z", "c")
HEAD = ("yh", "x")
LOG2E = math.log2(math.e)
CT = LOG2E / math.sqrt(TW)
CS = LOG2E / math.sqrt(SW)
TOK = 256
PACK = 384
F32 = jnp.float32
BF16 = jnp.bfloat16
NT = (((1,), (1,)), ((), ()))
PARAMS = pltpu.CompilerParams(vmem_limit_bytes=20 * 1024 * 1024)


def whole(n):
    return [pl.BlockSpec(memory_space=pltpu.VMEM)] * n


HBM = pl.BlockSpec(memory_space=pltpu.HBM)
SCALAR = pl.BlockSpec(memory_space=pltpu.SMEM)
TEACH, STUD = slice(0, TW), slice(TW, PACK)


def in_hbm(array):
    return pltpu.with_memory_space_constraint(array, pltpu.HBM)


def nt_dot(a, b):
    return lax.dot_general(a, b, NT, preferred_element_type=F32)


def prep_kernel(yl_ref, teach_in, stud_in, weight_in, own_ref, give_ref, teach_ref, stud_ref, weight_ref, sems):
    copies = [
        pltpu.make_async_copy(source, target, sems.at[i])
        for i, (source, target) in enumerate(
            ((teach_in, teach_ref), (stud_in, stud_ref), (weight_in, weight_ref))
        )
    ]
    for copy in copies:
        copy.start()
    for copy in copies:
        copy.wait()
    yl = yl_ref[0]
    weight = weight_ref[...]
    high = weight.astype(BF16).astype(F32)
    middle = (weight - high).astype(BF16).astype(F32)
    low = weight - high - middle
    row = lax.broadcasted_iota(jnp.int32, (16, TOK), 0)
    extra = jnp.where(row == 0, high, jnp.where(row == 1, middle, jnp.where(row == 2, low, 0.0)))
    packs = []
    for h in range(2):
        stud = stud_ref[h * SW : (h + 1) * SW, :].astype(F32)
        packs.append(jnp.concatenate([stud, extra], axis=0))
    first = yl == 0
    for ref, flip in ((own_ref, first), (give_ref, jnp.logical_not(first))):
        ref[:, TW:] = jnp.where(flip, packs[0], packs[1]).T.astype(BF16)
        ref[:, :TW] = jnp.where(flip, teach_ref[:, :TW].astype(F32), teach_ref[:, TW:].astype(F32)).astype(BF16)


def prepare(yl, teacher, stud_t, weights):
    packet = jax.ShapeDtypeStruct((TOK, PACK), BF16)
    return pl.pallas_call(
        prep_kernel,
        out_shape=(packet, packet),
        in_specs=[SCALAR] + [HBM] * 3,
        out_specs=tuple(whole(2)),
        scratch_shapes=[
            pltpu.VMEM((TOK, 2 * TW), BF16),
            pltpu.VMEM((2 * SW, TOK), BF16),
            pltpu.VMEM((1, TOK), F32),
            pltpu.SemaphoreType.DMA((3,)),
        ],
        compiler_params=PARAMS,
        name="prepare",
    )(yl, in_hbm(teacher), in_hbm(stud_t), in_hbm(weights))


def pair_kernel(own, sib, out):
    out[:TOK, :] = own[...]
    out[TOK:, :] = sib[...]


def pair_up(own, sib):
    return pl.pallas_call(
        pair_kernel,
        out_shape=jax.ShapeDtypeStruct((2 * TOK, PACK), BF16),
        in_specs=whole(2),
        out_specs=whole(1)[0],
        compiler_params=PARAMS,
        name="pair_up",
    )(own, sib)


def open_packets(pairs, held, weight_ref):
    lane = lax.broadcasted_iota(jnp.int32, (2 * TOK, PACK - TW), 1)
    for i, pair in enumerate(pairs):
        at = slice(2 * i * TOK, 2 * (i + 1) * TOK)
        held[at, :TW] = pair[:, :TW]
        stud = pair[:, TW:].astype(F32)
        held[at, TW:] = jnp.where(lane < SW, stud, 0.0).astype(BF16)
        columns = stud.T
        weight = columns[SW : SW + 1] + columns[SW + 1 : SW + 2] + columns[SW + 2 : SW + 3]
        weight_ref[0:1, at] = weight
        weight_ref[1:2, at] = jnp.log(weight) * LOG2E


def take_stats(held, key, before, out, last):
    for i in range(2):
        at = slice(2 * i * TOK, 2 * (i + 1) * TOK)
        t = nt_dot(key[:, TEACH], held[at, TEACH]).reshape(-1, 8, 2 * TOK) * CT
        s = nt_dot(key[:, STUD], held[at, STUD]).reshape(-1, 8, 2 * TOK) * CS
        t_max, s_max = jnp.max(t, axis=0), jnp.max(s, axis=0)
        if before is not None:
            state = [before[8 * k : 8 * k + 8, at] for k in range(5)]
            t_max, s_max = jnp.maximum(t_max, state[0]), jnp.maximum(s_max, state[3])
        t_exp = jnp.exp2(t - t_max[None])
        s_exp = jnp.exp2(s - s_max[None])
        t_sum, s_sum = jnp.sum(t_exp, axis=0), jnp.sum(s_exp, axis=0)
        cross = jnp.sum(t_exp * (t - s), axis=0)
        if before is not None:
            t_keep, s_keep = jnp.exp2(state[0] - t_max), jnp.exp2(state[3] - s_max)
            t_sum = t_sum + state[1] * t_keep
            cross = cross + state[2] * t_keep
            s_sum = s_sum + state[4] * s_keep
        if last:
            t_top = jnp.max(t_max, axis=0, keepdims=True)
            s_top = jnp.max(s_max, axis=0, keepdims=True)
            t_keep, s_keep = jnp.exp2(t_max - t_top), jnp.exp2(s_max - s_top)
            out[0:1, at] = t_top
            out[1:2, at] = jnp.sum(t_sum * t_keep, axis=0, keepdims=True)
            out[2:3, at] = jnp.sum(cross * t_keep, axis=0, keepdims=True)
            out[3:4, at] = s_top
            out[4:5, at] = jnp.sum(s_sum * s_keep, axis=0, keepdims=True)
        else:
            for k, value in enumerate((t_max, t_sum, cross, s_max, s_sum)):
                out[8 * k : 8 * k + 8, at] = value


def own_keys(held, columns):
    return jnp.concatenate([held[:TOK, columns], held[2 * TOK : 3 * TOK, columns]], axis=0)


def first_kernel(own_ref, got_ref, state, held, weight_ref):
    open_packets((own_ref, got_ref), held, weight_ref)
    take_stats(held, own_keys(held, slice(None)), None, state, False)


def more_kernel(last, held, key, before, out):
    take_stats(held, key, before, out, last)


def stat_cost(pairs):
    return pl.CostEstimate(flops=2 * pairs * 512, bytes_accessed=pairs * 4, transcendentals=2 * pairs)


def first_stats(own_pair, got_pair):
    return pl.pallas_call(
        first_kernel,
        out_shape=(
            jax.ShapeDtypeStruct((40, 4 * TOK), F32),
            jax.ShapeDtypeStruct((4 * TOK, PACK), BF16),
            jax.ShapeDtypeStruct((8, 4 * TOK), F32),
        ),
        in_specs=whole(2),
        out_specs=tuple(whole(3)),
        compiler_params=PARAMS,
        cost_estimate=stat_cost(4 * TOK * 2 * TOK),
        name="first_stats",
    )(own_pair, got_pair)


def more_stats(held, key, before, last=False):
    pairs = 4 * TOK * key.shape[0]
    return pl.pallas_call(
        functools.partial(more_kernel, last),
        out_shape=jax.ShapeDtypeStruct((8 if last else 40, 4 * TOK), F32),
        in_specs=whole(3),
        out_specs=whole(1)[0],
        input_output_aliases={} if last else {2: 0},
        compiler_params=PARAMS,
        cost_estimate=stat_cost(pairs),
        name="more_stats",
    )(held, key, before)


def merge_kernel(mine, sib, weight_ref, norm_ref, send_ref):
    total = jnp.zeros((1, TOK), F32)
    for i in range(4):
        at = slice(i * TOK, (i + 1) * TOK)
        there = slice((i ^ 1) * TOK, ((i ^ 1) + 1) * TOK)
        a = [mine[k : k + 1, at] for k in range(5)]
        b = [sib[k : k + 1, there] for k in range(5)]
        t_max, s_max = jnp.maximum(a[0], b[0]), jnp.maximum(a[3], b[3])
        ta, tb = jnp.exp2(a[0] - t_max), jnp.exp2(b[0] - t_max)
        sa, sb = jnp.exp2(a[3] - s_max), jnp.exp2(b[3] - s_max)
        t_sum, s_sum = a[1] * ta + b[1] * tb, a[4] * sa + b[4] * sb
        cross = a[2] * ta + b[2] * tb
        t_norm = t_max + jnp.log(t_sum) * LOG2E
        s_norm = s_max + jnp.log(s_sum) * LOG2E
        total = total + weight_ref[0:1, at] * (cross / t_sum - t_norm + s_norm)
        t_norm, s_norm = t_norm - weight_ref[1:2, at], s_norm - weight_ref[1:2, at]
        norm_ref[0:1, at] = t_norm
        norm_ref[1:2, at] = s_norm
        for z in range(8):
            send_ref[z, 0:1, at] = t_norm
            send_ref[z, 1:2, at] = s_norm
    loss = jnp.broadcast_to(jnp.sum(total, axis=1, keepdims=True), (2, 128))
    for z in range(8):
        send_ref[z, :, 4 * TOK :] = loss


def merge(mine, sib, weight):
    return pl.pallas_call(
        merge_kernel,
        out_shape=(jax.ShapeDtypeStruct((8, 4 * TOK), F32), jax.ShapeDtypeStruct((8, 2, 4 * TOK + 128), F32)),
        in_specs=whole(3),
        out_specs=tuple(whole(2)),
        compiler_params=PARAMS,
        name="merge",
    )(mine, sib, weight)


def column_of(row):
    return jnp.broadcast_to(row, (128, 128)).T


def slopes_of(t, s, t_norm, s_norm):
    return jnp.exp2(s - s_norm) - jnp.exp2(t - t_norm)


class Keys:
    def __init__(self, held, refs, late, sems):
        self.held, self.near, self.opposite, self.far, self.late = held, refs[:4], refs[4:6], refs[6:8], late
        self.copies = [pltpu.make_async_copy(self.far[i], late.at[i], sems.at[i]) for i in range(2)]

    def start(self):
        for copy in self.copies:
            copy.start()

    def wait(self):
        for copy in self.copies:
            copy.wait()

    def block(self, slot, columns):
        if slot == 0:
            return own_keys(self.held, columns)
        if slot <= 4:
            return self.near[slot - 1][:, columns]
        if slot == 5:
            return jnp.concatenate([self.opposite[0][:, columns], self.opposite[1][:, columns]], axis=0)
        return self.late[slot - 6, :, columns]

    def piece(self, i, columns):
        if i < 4:
            return self.near[i][:, columns]
        if i < 6:
            return self.held[(i - 4) * 2 * TOK : (i - 4) * 2 * TOK + TOK, columns]
        if i < 8:
            return self.opposite[i - 6][:, columns]
        return self.late[i - 8, :, columns]


STEPS = (0, 2, 2, 3, 3, 4, 1, 1)
KEY_SPECS = whole(6) + [HBM] * 2
KEY_SCRATCH = [pltpu.VMEM((2, 2 * TOK, PACK), BF16), pltpu.SemaphoreType.DMA((4,))]


def as_operands(packets):
    return [*packets[:6], *(in_hbm(p) for p in packets[6:])]


def row_kernel(held, norm_ref, *refs):
    result, t_norm, s_norm, out, late, sems = refs[8:]
    keys = Keys(held, refs[:8], late, sems)
    keys.start()
    for b in range(8):
        at = slice(b * 128, (b + 1) * 128)
        t_norm[at, :] = column_of(norm_ref[0:1, at])
        s_norm[at, :] = column_of(norm_ref[1:2, at])

    for half in range(2):
        at = slice(half * 2 * TOK, (half + 1) * 2 * TOK)
        tn, sn = t_norm[at, :], s_norm[at, :]
        for i in range(10):
            if i == 8 and half == 0:
                keys.wait()
            stud = keys.piece(i, STUD)
            t = nt_dot(held[at, TEACH], keys.piece(i, TEACH)) * CT
            s = nt_dot(held[at, STUD], stud) * CS
            p = jnp.concatenate(
                [slopes_of(t[:, k : k + 128], s[:, k : k + 128], tn, sn) for k in range(0, s.shape[1], 128)], axis=1
            )
            part = jnp.dot(p.astype(BF16), stud, preferred_element_type=F32)
            out[at, :] = part if i == 0 else out[at, :] + part
        pltpu.make_async_copy(out.at[at, :], result.at[at, :], sems.at[2 + half]).start()
    for half in range(2):
        at = slice(half * 2 * TOK, (half + 1) * 2 * TOK)
        pltpu.make_async_copy(out.at[at, :], result.at[at, :], sems.at[2 + half]).wait()


def row_part(held, norms, packets):
    pairs = 4 * TOK * 4096
    return pl.pallas_call(
        row_kernel,
        out_shape=pltpu.HBM((4 * TOK, 128), F32),
        in_specs=whole(2) + KEY_SPECS,
        out_specs=HBM,
        scratch_shapes=[pltpu.VMEM((4 * TOK, 128), F32)] * 3 + KEY_SCRATCH,
        compiler_params=PARAMS,
        cost_estimate=pl.CostEstimate(flops=2 * pairs * 640, bytes_accessed=pairs * 4, transcendentals=2 * pairs),
        name="row_part",
    )(held, norms, *as_operands(packets))


def col_kernel(query_at, place_ref, held, stat_ref, *refs):
    row_ref, keep, give = refs[8:11]
    acc, rows, late, sems = refs[-4:]
    if len(refs) == 16:
        total = jnp.sum(stat_ref[:, 0, 4 * TOK :], axis=0, keepdims=True)
        refs[11][...] = jnp.broadcast_to(total[None], (16, 1, 128))
    keys = Keys(held, refs[:8], late, sems)
    keys.start()
    at = slice(query_at, query_at + 2 * TOK)
    copy = pltpu.make_async_copy(row_ref.at[at, :], rows, sems.at[2])
    copy.start()
    toward = jnp.where(place_ref[0] == 0, 7, 1)
    for slot in range(8):
        if slot == 6:
            keys.wait()
            copy.wait()
        source = lax.rem(place_ref[1] + toward * STEPS[slot], 8)
        if slot in (0, 5):
            t_norm, s_norm = (
                jnp.concatenate([stat_ref[source, i : i + 1, k : k + TOK] for k in (0, 2 * TOK)], axis=1)
                for i in range(2)
            )
        else:
            plane = 2 * TOK * (1 - slot % 2 if slot < 5 else slot % 2)
            t_norm, s_norm = (stat_ref[source, i : i + 1, plane : plane + 2 * TOK] for i in range(2))
        stud = keys.block(slot, STUD)
        t = nt_dot(held[at, TEACH], keys.block(slot, TEACH)) * CT
        s = nt_dot(held[at, STUD], stud) * CS
        p = slopes_of(t, s, t_norm, s_norm).astype(BF16)
        part = jnp.dot(p, stud, preferred_element_type=F32)
        acc[...] = part if slot == 0 else acc[...] + part
    for i, out in enumerate((keep, give)):
        part = slice(i * TOK, (i + 1) * TOK)
        out[...] = (acc[part, :] + rows[part, :]).T[:SW, :] * (1.0 / math.sqrt(SW))


def col_part(place, held, stats, packets, rows, query_at, with_loss):
    pairs = 2 * TOK * 4096
    part = jax.ShapeDtypeStruct((SW, TOK), F32)
    return pl.pallas_call(
        functools.partial(col_kernel, query_at),
        out_shape=(part, part) + with_loss * (jax.ShapeDtypeStruct((16, 1, 128), F32),),
        in_specs=[SCALAR] + whole(2) + KEY_SPECS + [HBM],
        out_specs=tuple(whole(2 + with_loss)),
        scratch_shapes=[pltpu.VMEM((2 * TOK, 128), F32)] * 2 + KEY_SCRATCH,
        compiler_params=PARAMS,
        cost_estimate=pl.CostEstimate(flops=2 * pairs * 640, bytes_accessed=pairs * 4, transcendentals=2 * pairs),
        name="col_part",
    )(place, held, stats, *as_operands(packets), in_hbm(rows))


def onward(array):
    pairs = [(2 * z + c, 2 * ((z + (-1) ** c) % 8) + c) for z in range(8) for c in range(2)]
    return lax.ppermute(array, ("z", "c"), pairs)


def tied(*arrays):
    return lax.optimization_barrier(arrays)


def swap(array, axis):
    n = 4 if isinstance(axis, tuple) else 2
    return lax.ppermute(array, axis, [(i, n - 1 - i) for i in range(n)])


def local(teacher, student, weights):
    yl, z, c = lax.axis_index("yl"), lax.axis_index("z"), lax.axis_index("c")
    own, give = prepare(yl.reshape(1), teacher[0], student[0].T, weights.reshape(1, TOK))
    got = swap(give, "yl")
    own_pair = pair_up(own, swap(own, "c"))
    a1 = onward(own_pair)
    got_pair = pair_up(got, swap(got, "c"))
    a1, sent_pair = tied(a1, got_pair)
    b1 = onward(sent_pair)
    a2 = onward(a1)
    state, held, weight = first_stats(own_pair, got_pair)
    b1, state = tied(b1, state)
    b2 = onward(b1)
    state = more_stats(held, a1, state)
    a2, state = tied(a2, state)
    a3 = onward(a2)
    state = more_stats(held, b1, state)
    b2, state = tied(b2, state)
    b3 = onward(b2)
    state = more_stats(held, a2, state)
    a3, state = tied(a3, state)
    a4 = onward(a3[:TOK])
    state = more_stats(held, b2, state)
    b3, state = tied(b3, state)
    b4 = onward(b3[:TOK])
    for packets in (a3, b3, a4):
        state = more_stats(held, packets, state)
    state = more_stats(held, b4, state, last=True)
    packets = (a2, b2, a3, b3, a4, b4, a1, b1)
    norms, send = merge(state, swap(state, "c"), weight)
    stats = lax.all_to_all(send, "z", 0, 0, tiled=True)
    rows = row_part(held, norms, packets)
    place = jnp.stack([c, z])
    far_keep, far_give, loss = col_part(place, held, stats, packets, rows, 2 * TOK, True)
    losses = lax.all_to_all(loss, ("yl", *HEAD), 0, 0, tiled=True)
    other = swap(far_keep, "yl") + swap(far_give, ("yl", "c"))
    rows, other = tied(rows, other)
    near_keep, near_give = col_part(place, held, stats, packets, rows, 0, False)
    mine = near_keep + swap(near_give, "c")
    grad = jnp.where(yl == 0, jnp.concatenate([mine, other]), jnp.concatenate([other, mine]))
    mean_loss = jnp.sum(losses[:, 0, 0]) * (math.log(2.0) / (HEADS * 8192))
    return mean_loss, grad.T[None]


def solution(mesh):
    finer = Mesh(mesh.devices.reshape(2, 8, 2, 2, 4), ("yl", "z", "c", "yh", "x"))
    return jax.shard_map(
        local,
        mesh=finer,
        in_specs=(P(None, SEQ, HEAD), P(None, SEQ, HEAD), P(SEQ)),
        out_specs=(P(), P(None, SEQ, HEAD)),
        check_vma=False,
    )
```

```python
import functools
import math

import jax
import jax.numpy as jnp
from jax import lax
from jax.experimental import pallas as pl
from jax.experimental.pallas import tpu as pltpu
from jax.sharding import Mesh
from jax.sharding import PartitionSpec as P

TW = 256
SW = 112
HEADS = 16
SEQ = ("yl", "z", "c")
HEAD = ("yh", "x")
LOG2E = math.log2(math.e)
CT = LOG2E / math.sqrt(TW)
CS = LOG2E / math.sqrt(SW)
TOK = 256
PACK = 384
F32 = jnp.float32
BF16 = jnp.bfloat16
NT = (((1,), (1,)), ((), ()))
PARAMS = pltpu.CompilerParams(vmem_limit_bytes=20 * 1024 * 1024)


def whole(n):
    return [pl.BlockSpec(memory_space=pltpu.VMEM)] * n


HBM = pl.BlockSpec(memory_space=pltpu.HBM)
SCALAR = pl.BlockSpec(memory_space=pltpu.SMEM)
TEACH, STUD = slice(0, TW), slice(TW, PACK)


def in_hbm(array):
    return pltpu.with_memory_space_constraint(array, pltpu.HBM)


def nt_dot(a, b):
    return lax.dot_general(a, b, NT, preferred_element_type=F32)


def prep_kernel(yl_ref, teach_in, stud_in, weight_in, own_ref, give_ref, teach_ref, stud_ref, weight_ref, sems):
    copies = [
        pltpu.make_async_copy(source, target, sems.at[i])
        for i, (source, target) in enumerate(
            ((teach_in, teach_ref), (stud_in, stud_ref), (weight_in, weight_ref))
        )
    ]
    for copy in copies:
        copy.start()
    for copy in copies:
        copy.wait()
    yl = yl_ref[0]
    weight = weight_ref[...]
    high = weight.astype(BF16).astype(F32)
    middle = (weight - high).astype(BF16).astype(F32)
    low = weight - high - middle
    row = lax.broadcasted_iota(jnp.int32, (16, TOK), 0)
    extra = jnp.where(row == 0, high, jnp.where(row == 1, middle, jnp.where(row == 2, low, 0.0)))
    packs = []
    for h in range(2):
        stud = stud_ref[h * SW : (h + 1) * SW, :].astype(F32)
        packs.append(jnp.concatenate([stud, extra], axis=0))
    first = yl == 0
    for ref, flip in ((own_ref, first), (give_ref, jnp.logical_not(first))):
        ref[:, TW:] = jnp.where(flip, packs[0], packs[1]).T.astype(BF16)
        ref[:, :TW] = jnp.where(flip, teach_ref[:, :TW].astype(F32), teach_ref[:, TW:].astype(F32)).astype(BF16)


def prepare(yl, teacher, stud_t, weights):
    packet = jax.ShapeDtypeStruct((TOK, PACK), BF16)
    return pl.pallas_call(
        prep_kernel,
        out_shape=(packet, packet),
        in_specs=[SCALAR] + [HBM] * 3,
        out_specs=tuple(whole(2)),
        scratch_shapes=[
            pltpu.VMEM((TOK, 2 * TW), BF16),
            pltpu.VMEM((2 * SW, TOK), BF16),
            pltpu.VMEM((1, TOK), F32),
            pltpu.SemaphoreType.DMA((3,)),
        ],
        compiler_params=PARAMS,
        name="prepare",
    )(yl, in_hbm(teacher), in_hbm(stud_t), in_hbm(weights))


def pair_kernel(own, sib, out):
    out[:TOK, :] = own[...]
    out[TOK:, :] = sib[...]


def pair_up(own, sib):
    return pl.pallas_call(
        pair_kernel,
        out_shape=jax.ShapeDtypeStruct((2 * TOK, PACK), BF16),
        in_specs=whole(2),
        out_specs=whole(1)[0],
        compiler_params=PARAMS,
        name="pair_up",
    )(own, sib)


def open_packets(pairs, held, weight_ref):
    lane = lax.broadcasted_iota(jnp.int32, (2 * TOK, PACK - TW), 1)
    for i, pair in enumerate(pairs):
        at = slice(2 * i * TOK, 2 * (i + 1) * TOK)
        held[at, :TW] = pair[:, :TW]
        stud = pair[:, TW:].astype(F32)
        held[at, TW:] = jnp.where(lane < SW, stud, 0.0).astype(BF16)
        columns = stud.T
        weight = columns[SW : SW + 1] + columns[SW + 1 : SW + 2] + columns[SW + 2 : SW + 3]
        weight_ref[0:1, at] = weight
        weight_ref[1:2, at] = jnp.log(weight) * LOG2E


def take_stats(held, key, before, out, last):
    for i in range(2):
        at = slice(2 * i * TOK, 2 * (i + 1) * TOK)
        t = nt_dot(key[:, TEACH], held[at, TEACH]).reshape(-1, 8, 2 * TOK) * CT
        s = nt_dot(key[:, STUD], held[at, STUD]).reshape(-1, 8, 2 * TOK) * CS
        t_max, s_max = jnp.max(t, axis=0), jnp.max(s, axis=0)
        if before is not None:
            state = [before[8 * k : 8 * k + 8, at] for k in range(5)]
            t_max, s_max = jnp.maximum(t_max, state[0]), jnp.maximum(s_max, state[3])
        t_exp = jnp.exp2(t - t_max[None])
        s_exp = jnp.exp2(s - s_max[None])
        t_sum, s_sum = jnp.sum(t_exp, axis=0), jnp.sum(s_exp, axis=0)
        cross = jnp.sum(t_exp * (t - s), axis=0)
        if before is not None:
            t_keep, s_keep = jnp.exp2(state[0] - t_max), jnp.exp2(state[3] - s_max)
            t_sum = t_sum + state[1] * t_keep
            cross = cross + state[2] * t_keep
            s_sum = s_sum + state[4] * s_keep
        if last:
            t_top = jnp.max(t_max, axis=0, keepdims=True)
            s_top = jnp.max(s_max, axis=0, keepdims=True)
            t_keep, s_keep = jnp.exp2(t_max - t_top), jnp.exp2(s_max - s_top)
            out[0:1, at] = t_top
            out[1:2, at] = jnp.sum(t_sum * t_keep, axis=0, keepdims=True)
            out[2:3, at] = jnp.sum(cross * t_keep, axis=0, keepdims=True)
            out[3:4, at] = s_top
            out[4:5, at] = jnp.sum(s_sum * s_keep, axis=0, keepdims=True)
        else:
            for k, value in enumerate((t_max, t_sum, cross, s_max, s_sum)):
                out[8 * k : 8 * k + 8, at] = value


def own_keys(held, columns):
    return jnp.concatenate([held[:TOK, columns], held[2 * TOK : 3 * TOK, columns]], axis=0)


def first_kernel(own_ref, got_ref, state, held, weight_ref):
    open_packets((own_ref, got_ref), held, weight_ref)
    take_stats(held, own_keys(held, slice(None)), None, state, False)


def more_kernel(last, held, key, before, out):
    take_stats(held, key, before, out, last)


def stat_cost(pairs):
    return pl.CostEstimate(flops=2 * pairs * 512, bytes_accessed=pairs * 4, transcendentals=2 * pairs)


def first_stats(own_pair, got_pair):
    return pl.pallas_call(
        first_kernel,
        out_shape=(
            jax.ShapeDtypeStruct((40, 4 * TOK), F32),
            jax.ShapeDtypeStruct((4 * TOK, PACK), BF16),
            jax.ShapeDtypeStruct((8, 4 * TOK), F32),
        ),
        in_specs=whole(2),
        out_specs=tuple(whole(3)),
        compiler_params=PARAMS,
        cost_estimate=stat_cost(4 * TOK * 2 * TOK),
        name="first_stats",
    )(own_pair, got_pair)


def more_stats(held, key, before, last=False):
    pairs = 4 * TOK * key.shape[0]
    return pl.pallas_call(
        functools.partial(more_kernel, last),
        out_shape=jax.ShapeDtypeStruct((8 if last else 40, 4 * TOK), F32),
        in_specs=whole(3),
        out_specs=whole(1)[0],
        input_output_aliases={} if last else {2: 0},
        compiler_params=PARAMS,
        cost_estimate=stat_cost(pairs),
        name="more_stats",
    )(held, key, before)


def merge_kernel(mine, sib, weight_ref, norm_ref, send_ref):
    total = jnp.zeros((1, TOK), F32)
    for i in range(4):
        at = slice(i * TOK, (i + 1) * TOK)
        there = slice((i ^ 1) * TOK, ((i ^ 1) + 1) * TOK)
        a = [mine[k : k + 1, at] for k in range(5)]
        b = [sib[k : k + 1, there] for k in range(5)]
        t_max, s_max = jnp.maximum(a[0], b[0]), jnp.maximum(a[3], b[3])
        ta, tb = jnp.exp2(a[0] - t_max), jnp.exp2(b[0] - t_max)
        sa, sb = jnp.exp2(a[3] - s_max), jnp.exp2(b[3] - s_max)
        t_sum, s_sum = a[1] * ta + b[1] * tb, a[4] * sa + b[4] * sb
        cross = a[2] * ta + b[2] * tb
        t_norm = t_max + jnp.log(t_sum) * LOG2E
        s_norm = s_max + jnp.log(s_sum) * LOG2E
        total = total + weight_ref[0:1, at] * (cross / t_sum - t_norm + s_norm)
        t_norm, s_norm = t_norm - weight_ref[1:2, at], s_norm - weight_ref[1:2, at]
        norm_ref[0:1, at] = t_norm
        norm_ref[1:2, at] = s_norm
        for z in range(8):
            send_ref[z, 0:1, at] = t_norm
            send_ref[z, 1:2, at] = s_norm
    loss = jnp.broadcast_to(jnp.sum(total, axis=1, keepdims=True), (2, 128))
    for z in range(8):
        send_ref[z, :, 4 * TOK :] = loss


def merge(mine, sib, weight):
    return pl.pallas_call(
        merge_kernel,
        out_shape=(jax.ShapeDtypeStruct((8, 4 * TOK), F32), jax.ShapeDtypeStruct((8, 2, 4 * TOK + 128), F32)),
        in_specs=whole(3),
        out_specs=tuple(whole(2)),
        compiler_params=PARAMS,
        name="merge",
    )(mine, sib, weight)


def column_of(row):
    return jnp.broadcast_to(row, (128, 128)).T


def slopes_of(t, s, t_norm, s_norm):
    return jnp.exp2(s - s_norm) - jnp.exp2(t - t_norm)


class Keys:
    def __init__(self, held, refs, late, sems):
        self.held, self.near, self.opposite, self.far, self.late = held, refs[:4], refs[4:6], refs[6:8], late
        self.copies = [pltpu.make_async_copy(self.far[i], late.at[i], sems.at[i]) for i in range(2)]

    def start(self):
        for copy in self.copies:
            copy.start()

    def wait(self):
        for copy in self.copies:
            copy.wait()

    def block(self, slot, columns):
        if slot == 0:
            return own_keys(self.held, columns)
        if slot <= 4:
            return self.near[slot - 1][:, columns]
        if slot == 5:
            return jnp.concatenate([self.opposite[0][:, columns], self.opposite[1][:, columns]], axis=0)
        return self.late[slot - 6, :, columns]

    def piece(self, i, columns):
        if i < 4:
            return self.near[i][:, columns]
        if i < 6:
            return self.held[(i - 4) * 2 * TOK : (i - 4) * 2 * TOK + TOK, columns]
        if i < 8:
            return self.opposite[i - 6][:, columns]
        return self.late[i - 8, :, columns]


STEPS = (0, 2, 2, 3, 3, 4, 1, 1)
KEY_SPECS = whole(6) + [HBM] * 2
KEY_SCRATCH = [pltpu.VMEM((2, 2 * TOK, PACK), BF16), pltpu.SemaphoreType.DMA((4,))]


def as_operands(packets):
    return [*packets[:6], *(in_hbm(p) for p in packets[6:])]


def row_kernel(held, norm_ref, *refs):
    result, t_norm, s_norm, out, late, sems = refs[8:]
    keys = Keys(held, refs[:8], late, sems)
    keys.start()
    for b in range(8):
        at = slice(b * 128, (b + 1) * 128)
        t_norm[at, :] = column_of(norm_ref[0:1, at])
        s_norm[at, :] = column_of(norm_ref[1:2, at])

    def step(half, carry):
        at = pl.ds(pl.multiple_of(half * 2 * TOK, 2 * TOK), 2 * TOK)
        tn, sn = t_norm[at, :], s_norm[at, :]
        for i in range(10):
            if i == 8:
                pl.when(half == 0)(keys.wait)
            stud = keys.piece(i, STUD)
            t = nt_dot(held[at, TEACH], keys.piece(i, TEACH)) * CT
            s = nt_dot(held[at, STUD], stud) * CS
            p = jnp.concatenate(
                [slopes_of(t[:, k : k + 128], s[:, k : k + 128], tn, sn) for k in range(0, s.shape[1], 128)], axis=1
            )
            part = jnp.dot(p.astype(BF16), stud, preferred_element_type=F32)
            out[at, :] = part if i == 0 else out[at, :] + part
        pltpu.make_async_copy(out.at[at, :], result.at[at, :], sems.at[2 + half]).start()
        return carry

    lax.fori_loop(0, 2, step, 0)
    for half in range(2):
        at = slice(half * 2 * TOK, (half + 1) * 2 * TOK)
        pltpu.make_async_copy(out.at[at, :], result.at[at, :], sems.at[2 + half]).wait()


def row_part(held, norms, packets):
    pairs = 4 * TOK * 4096
    return pl.pallas_call(
        row_kernel,
        out_shape=pltpu.HBM((4 * TOK, 128), F32),
        in_specs=whole(2) + KEY_SPECS,
        out_specs=HBM,
        scratch_shapes=[pltpu.VMEM((4 * TOK, 128), F32)] * 3 + KEY_SCRATCH,
        compiler_params=PARAMS,
        cost_estimate=pl.CostEstimate(flops=2 * pairs * 640, bytes_accessed=pairs * 4, transcendentals=2 * pairs),
        name="row_part",
    )(held, norms, *as_operands(packets))


def col_kernel(query_at, place_ref, held, stat_ref, *refs):
    row_ref, keep, give = refs[8:11]
    acc, rows, late, sems = refs[-4:]
    if len(refs) == 16:
        total = jnp.sum(stat_ref[:, 0, 4 * TOK :], axis=0, keepdims=True)
        refs[11][...] = jnp.broadcast_to(total[None], (16, 1, 128))
    keys = Keys(held, refs[:8], late, sems)
    keys.start()
    at = slice(query_at, query_at + 2 * TOK)
    copy = pltpu.make_async_copy(row_ref.at[at, :], rows, sems.at[2])
    copy.start()
    toward = jnp.where(place_ref[0] == 0, 7, 1)
    for slot in range(8):
        if slot == 6:
            keys.wait()
            copy.wait()
        source = lax.rem(place_ref[1] + toward * STEPS[slot], 8)
        if slot in (0, 5):
            t_norm, s_norm = (
                jnp.concatenate([stat_ref[source, i : i + 1, k : k + TOK] for k in (0, 2 * TOK)], axis=1)
                for i in range(2)
            )
        else:
            plane = 2 * TOK * (1 - slot % 2 if slot < 5 else slot % 2)
            t_norm, s_norm = (stat_ref[source, i : i + 1, plane : plane + 2 * TOK] for i in range(2))
        stud = keys.block(slot, STUD)
        t = nt_dot(held[at, TEACH], keys.block(slot, TEACH)) * CT
        s = nt_dot(held[at, STUD], stud) * CS
        p = slopes_of(t, s, t_norm, s_norm).astype(BF16)
        part = jnp.dot(p, stud, preferred_element_type=F32)
        acc[...] = part if slot == 0 else acc[...] + part
    for i, out in enumerate((keep, give)):
        part = slice(i * TOK, (i + 1) * TOK)
        out[...] = (acc[part, :] + rows[part, :]).T[:SW, :] * (1.0 / math.sqrt(SW))


def col_part(place, held, stats, packets, rows, query_at, with_loss):
    pairs = 2 * TOK * 4096
    part = jax.ShapeDtypeStruct((SW, TOK), F32)
    return pl.pallas_call(
        functools.partial(col_kernel, query_at),
        out_shape=(part, part) + with_loss * (jax.ShapeDtypeStruct((16, 1, 128), F32),),
        in_specs=[SCALAR] + whole(2) + KEY_SPECS + [HBM],
        out_specs=tuple(whole(2 + with_loss)),
        scratch_shapes=[pltpu.VMEM((2 * TOK, 128), F32)] * 2 + KEY_SCRATCH,
        compiler_params=PARAMS,
        cost_estimate=pl.CostEstimate(flops=2 * pairs * 640, bytes_accessed=pairs * 4, transcendentals=2 * pairs),
        name="col_part",
    )(place, held, stats, *as_operands(packets), in_hbm(rows))


def onward(array):
    pairs = [(2 * z + c, 2 * ((z + (-1) ** c) % 8) + c) for z in range(8) for c in range(2)]
    return lax.ppermute(array, ("z", "c"), pairs)


def tied(*arrays):
    return lax.optimization_barrier(arrays)


def swap(array, axis):
    n = 4 if isinstance(axis, tuple) else 2
    return lax.ppermute(array, axis, [(i, n - 1 - i) for i in range(n)])


def local(teacher, student, weights):
    yl, z, c = lax.axis_index("yl"), lax.axis_index("z"), lax.axis_index("c")
    own, give = prepare(yl.reshape(1), teacher[0], student[0].T, weights.reshape(1, TOK))
    got = swap(give, "yl")
    own_pair = pair_up(own, swap(own, "c"))
    a1 = onward(own_pair)
    got_pair = pair_up(got, swap(got, "c"))
    a1, sent_pair = tied(a1, got_pair)
    b1 = onward(sent_pair)
    a2 = onward(a1)
    state, held, weight = first_stats(own_pair, got_pair)
    b1, state = tied(b1, state)
    b2 = onward(b1)
    state = more_stats(held, a1, state)
    a2, state = tied(a2, state)
    a3 = onward(a2)
    state = more_stats(held, b1, state)
    b2, state = tied(b2, state)
    b3 = onward(b2)
    state = more_stats(held, a2, state)
    a3, state = tied(a3, state)
    a4 = onward(a3[:TOK])
    state = more_stats(held, b2, state)
    b3, state = tied(b3, state)
    b4 = onward(b3[:TOK])
    for packets in (a3, b3, a4):
        state = more_stats(held, packets, state)
    state = more_stats(held, b4, state, last=True)
    packets = (a2, b2, a3, b3, a4, b4, a1, b1)
    norms, send = merge(state, swap(state, "c"), weight)
    stats = lax.all_to_all(send, "z", 0, 0, tiled=True)
    rows = row_part(held, norms, packets)
    place = jnp.stack([c, z])
    far_keep, far_give, loss = col_part(place, held, stats, packets, rows, 2 * TOK, True)
    losses = lax.all_to_all(loss, ("yl", *HEAD), 0, 0, tiled=True)
    other = swap(far_keep, "yl") + swap(far_give, ("yl", "c"))
    rows, other = tied(rows, other)
    near_keep, near_give = col_part(place, held, stats, packets, rows, 0, False)
    mine = near_keep + swap(near_give, "c")
    grad = jnp.where(yl == 0, jnp.concatenate([mine, other]), jnp.concatenate([other, mine]))
    mean_loss = jnp.sum(losses[:, 0, 0]) * (math.log(2.0) / (HEADS * 8192))
    return mean_loss, grad.T[None]


def solution(mesh):
    finer = Mesh(mesh.devices.reshape(2, 8, 2, 2, 4), ("yl", "z", "c", "yh", "x"))
    return jax.shard_map(
        local,
        mesh=finer,
        in_specs=(P(None, SEQ, HEAD), P(None, SEQ, HEAD), P(SEQ)),
        out_specs=(P(), P(None, SEQ, HEAD)),
        check_vma=False,
    )
```

```python
import functools
import math

import jax
import jax.numpy as jnp
from jax import lax
from jax.experimental import pallas as pl
from jax.experimental.pallas import tpu as pltpu
from jax.sharding import Mesh
from jax.sharding import PartitionSpec as P

TW = 256
SW = 112
HEADS = 16
SEQ = ("yl", "z", "c")
HEAD = ("yh", "x")
LOG2E = math.log2(math.e)
CT = LOG2E / math.sqrt(TW)
CS = LOG2E / math.sqrt(SW)
TOK = 256
PACK = 384
F32 = jnp.float32
BF16 = jnp.bfloat16
NT = (((1,), (1,)), ((), ()))
PARAMS = pltpu.CompilerParams(vmem_limit_bytes=20 * 1024 * 1024)


def whole(n):
    return [pl.BlockSpec(memory_space=pltpu.VMEM)] * n


HBM = pl.BlockSpec(memory_space=pltpu.HBM)
SCALAR = pl.BlockSpec(memory_space=pltpu.SMEM)
TEACH, STUD = slice(0, TW), slice(TW, PACK)


def in_hbm(array):
    return pltpu.with_memory_space_constraint(array, pltpu.HBM)


def nt_dot(a, b):
    return lax.dot_general(a, b, NT, preferred_element_type=F32)


def prep_kernel(yl_ref, teach_in, stud_in, weight_in, own_ref, give_ref, teach_ref, stud_ref, weight_ref, sems):
    copies = [
        pltpu.make_async_copy(source, target, sems.at[i])
        for i, (source, target) in enumerate(
            ((teach_in, teach_ref), (stud_in, stud_ref), (weight_in, weight_ref))
        )
    ]
    for copy in copies:
        copy.start()
    for copy in copies:
        copy.wait()
    yl = yl_ref[0]
    weight = weight_ref[...]
    high = weight.astype(BF16).astype(F32)
    middle = (weight - high).astype(BF16).astype(F32)
    low = weight - high - middle
    row = lax.broadcasted_iota(jnp.int32, (16, TOK), 0)
    extra = jnp.where(row == 0, high, jnp.where(row == 1, middle, jnp.where(row == 2, low, 0.0)))
    packs = []
    for h in range(2):
        stud = stud_ref[h * SW : (h + 1) * SW, :].astype(F32)
        packs.append(jnp.concatenate([stud, extra], axis=0))
    first = yl == 0
    for ref, flip in ((own_ref, first), (give_ref, jnp.logical_not(first))):
        ref[:, TW:] = jnp.where(flip, packs[0], packs[1]).T.astype(BF16)
        ref[:, :TW] = jnp.where(flip, teach_ref[:, :TW].astype(F32), teach_ref[:, TW:].astype(F32)).astype(BF16)


def prepare(yl, teacher, stud_t, weights):
    packet = jax.ShapeDtypeStruct((TOK, PACK), BF16)
    return pl.pallas_call(
        prep_kernel,
        out_shape=(packet, packet),
        in_specs=[SCALAR] + [HBM] * 3,
        out_specs=tuple(whole(2)),
        scratch_shapes=[
            pltpu.VMEM((TOK, 2 * TW), BF16),
            pltpu.VMEM((2 * SW, TOK), BF16),
            pltpu.VMEM((1, TOK), F32),
            pltpu.SemaphoreType.DMA((3,)),
        ],
        compiler_params=PARAMS,
        name="prepare",
    )(yl, in_hbm(teacher), in_hbm(stud_t), in_hbm(weights))


def pair_kernel(own, sib, out):
    out[:TOK, :] = own[...]
    out[TOK:, :] = sib[...]


def pair_up(own, sib):
    return pl.pallas_call(
        pair_kernel,
        out_shape=jax.ShapeDtypeStruct((2 * TOK, PACK), BF16),
        in_specs=whole(2),
        out_specs=whole(1)[0],
        compiler_params=PARAMS,
        name="pair_up",
    )(own, sib)


def open_packets(pairs, held, weight_ref):
    lane = lax.broadcasted_iota(jnp.int32, (2 * TOK, PACK - TW), 1)
    for i, pair in enumerate(pairs):
        at = slice(2 * i * TOK, 2 * (i + 1) * TOK)
        held[at, :TW] = pair[:, :TW]
        stud = pair[:, TW:].astype(F32)
        held[at, TW:] = jnp.where(lane < SW, stud, 0.0).astype(BF16)
        columns = stud.T
        weight = columns[SW : SW + 1] + columns[SW + 1 : SW + 2] + columns[SW + 2 : SW + 3]
        weight_ref[0:1, at] = weight
        weight_ref[1:2, at] = jnp.log(weight) * LOG2E


def take_stats(held, key, before, out, last):
    for i in range(2):
        at = slice(2 * i * TOK, 2 * (i + 1) * TOK)
        t = nt_dot(key[:, TEACH], held[at, TEACH]).reshape(-1, 8, 2 * TOK) * CT
        s = nt_dot(key[:, STUD], held[at, STUD]).reshape(-1, 8, 2 * TOK) * CS
        t_max, s_max = jnp.max(t, axis=0), jnp.max(s, axis=0)
        if before is not None:
            state = [before[8 * k : 8 * k + 8, at] for k in range(5)]
            t_max, s_max = jnp.maximum(t_max, state[0]), jnp.maximum(s_max, state[3])
        t_exp = jnp.exp2(t - t_max[None])
        s_exp = jnp.exp2(s - s_max[None])
        t_sum, s_sum = jnp.sum(t_exp, axis=0), jnp.sum(s_exp, axis=0)
        cross = jnp.sum(t_exp * (t - s), axis=0)
        if before is not None:
            t_keep, s_keep = jnp.exp2(state[0] - t_max), jnp.exp2(state[3] - s_max)
            t_sum = t_sum + state[1] * t_keep
            cross = cross + state[2] * t_keep
            s_sum = s_sum + state[4] * s_keep
        if last:
            t_top = jnp.max(t_max, axis=0, keepdims=True)
            s_top = jnp.max(s_max, axis=0, keepdims=True)
            t_keep, s_keep = jnp.exp2(t_max - t_top), jnp.exp2(s_max - s_top)
            out[0:1, at] = t_top
            out[1:2, at] = jnp.sum(t_sum * t_keep, axis=0, keepdims=True)
            out[2:3, at] = jnp.sum(cross * t_keep, axis=0, keepdims=True)
            out[3:4, at] = s_top
            out[4:5, at] = jnp.sum(s_sum * s_keep, axis=0, keepdims=True)
        else:
            for k, value in enumerate((t_max, t_sum, cross, s_max, s_sum)):
                out[8 * k : 8 * k + 8, at] = value


def own_keys(held, columns):
    return jnp.concatenate([held[:TOK, columns], held[2 * TOK : 3 * TOK, columns]], axis=0)


def first_kernel(own_ref, got_ref, state, held, weight_ref):
    open_packets((own_ref, got_ref), held, weight_ref)
    take_stats(held, own_keys(held, slice(None)), None, state, False)


def more_kernel(last, held, key, before, out):
    take_stats(held, key, before, out, last)


def stat_cost(pairs):
    return pl.CostEstimate(flops=2 * pairs * 512, bytes_accessed=pairs * 4, transcendentals=2 * pairs)


def first_stats(own_pair, got_pair):
    return pl.pallas_call(
        first_kernel,
        out_shape=(
            jax.ShapeDtypeStruct((40, 4 * TOK), F32),
            jax.ShapeDtypeStruct((4 * TOK, PACK), BF16),
            jax.ShapeDtypeStruct((8, 4 * TOK), F32),
        ),
        in_specs=whole(2),
        out_specs=tuple(whole(3)),
        compiler_params=PARAMS,
        cost_estimate=stat_cost(4 * TOK * 2 * TOK),
        name="first_stats",
    )(own_pair, got_pair)


def more_stats(held, key, before, last=False):
    pairs = 4 * TOK * key.shape[0]
    return pl.pallas_call(
        functools.partial(more_kernel, last),
        out_shape=jax.ShapeDtypeStruct((8 if last else 40, 4 * TOK), F32),
        in_specs=whole(3),
        out_specs=whole(1)[0],
        input_output_aliases={} if last else {2: 0},
        compiler_params=PARAMS,
        cost_estimate=stat_cost(pairs),
        name="more_stats",
    )(held, key, before)


def merge_kernel(mine, sib, weight_ref, norm_ref, send_ref):
    total = jnp.zeros((1, TOK), F32)
    for i in range(4):
        at = slice(i * TOK, (i + 1) * TOK)
        there = slice((i ^ 1) * TOK, ((i ^ 1) + 1) * TOK)
        a = [mine[k : k + 1, at] for k in range(5)]
        b = [sib[k : k + 1, there] for k in range(5)]
        t_max, s_max = jnp.maximum(a[0], b[0]), jnp.maximum(a[3], b[3])
        ta, tb = jnp.exp2(a[0] - t_max), jnp.exp2(b[0] - t_max)
        sa, sb = jnp.exp2(a[3] - s_max), jnp.exp2(b[3] - s_max)
        t_sum, s_sum = a[1] * ta + b[1] * tb, a[4] * sa + b[4] * sb
        cross = a[2] * ta + b[2] * tb
        t_norm = t_max + jnp.log(t_sum) * LOG2E
        s_norm = s_max + jnp.log(s_sum) * LOG2E
        total = total + weight_ref[0:1, at] * (cross / t_sum - t_norm + s_norm)
        t_norm, s_norm = t_norm - weight_ref[1:2, at], s_norm - weight_ref[1:2, at]
        norm_ref[0:1, at] = t_norm
        norm_ref[1:2, at] = s_norm
        for z in range(8):
            send_ref[z, 0:1, at] = t_norm
            send_ref[z, 1:2, at] = s_norm
    loss = jnp.broadcast_to(jnp.sum(total, axis=1, keepdims=True), (2, 128))
    for z in range(8):
        send_ref[z, :, 4 * TOK :] = loss


def merge(mine, sib, weight):
    return pl.pallas_call(
        merge_kernel,
        out_shape=(jax.ShapeDtypeStruct((8, 4 * TOK), F32), jax.ShapeDtypeStruct((8, 2, 4 * TOK + 128), F32)),
        in_specs=whole(3),
        out_specs=tuple(whole(2)),
        compiler_params=PARAMS,
        name="merge",
    )(mine, sib, weight)


def column_of(row):
    return jnp.broadcast_to(row, (128, 128)).T


def slopes_of(t, s, t_norm, s_norm):
    return jnp.exp2(s - s_norm) - jnp.exp2(t - t_norm)


class Keys:
    def __init__(self, held, refs, late, sems):
        self.held, self.near, self.opposite, self.far, self.late = held, refs[:4], refs[4:6], refs[6:8], late
        self.copies = [pltpu.make_async_copy(self.far[0], late.at[0], sems.at[0])]

    def start(self):
        for copy in self.copies:
            copy.start()

    def wait(self):
        for copy in self.copies:
            copy.wait()

    def block(self, slot, columns):
        if slot == 0:
            return own_keys(self.held, columns)
        if slot <= 4:
            return self.near[slot - 1][:, columns]
        if slot == 5:
            return jnp.concatenate([self.opposite[0][:, columns], self.opposite[1][:, columns]], axis=0)
        return self.late[0, :, columns] if slot == 6 else self.far[1][:, columns]

    def piece(self, i, columns):
        if i < 4:
            return self.near[i][:, columns]
        if i < 6:
            return self.held[(i - 4) * 2 * TOK : (i - 4) * 2 * TOK + TOK, columns]
        if i < 8:
            return self.opposite[i - 6][:, columns]
        return self.late[0, :, columns] if i == 8 else self.far[1][:, columns]


STEPS = (0, 2, 2, 3, 3, 4, 1, 1)
KEY_SPECS = whole(6) + [HBM] + whole(1)
KEY_SCRATCH = [pltpu.VMEM((1, 2 * TOK, PACK), BF16), pltpu.SemaphoreType.DMA((4,))]


def as_operands(packets):
    return [*packets[:6], in_hbm(packets[6]), packets[7]]


def row_kernel(held, norm_ref, *refs):
    result, t_norm, s_norm, out, late, sems = refs[8:]
    keys = Keys(held, refs[:8], late, sems)
    keys.start()
    for b in range(8):
        at = slice(b * 128, (b + 1) * 128)
        t_norm[at, :] = column_of(norm_ref[0:1, at])
        s_norm[at, :] = column_of(norm_ref[1:2, at])

    def step(half, carry):
        at = pl.ds(pl.multiple_of(half * 2 * TOK, 2 * TOK), 2 * TOK)
        tn, sn = t_norm[at, :], s_norm[at, :]
        for i in range(10):
            if i == 8:
                pl.when(half == 0)(keys.wait)
            stud = keys.piece(i, STUD)
            t = nt_dot(held[at, TEACH], keys.piece(i, TEACH)) * CT
            s = nt_dot(held[at, STUD], stud) * CS
            p = jnp.concatenate(
                [slopes_of(t[:, k : k + 128], s[:, k : k + 128], tn, sn) for k in range(0, s.shape[1], 128)], axis=1
            )
            part = jnp.dot(p.astype(BF16), stud, preferred_element_type=F32)
            out[at, :] = part if i == 0 else out[at, :] + part
        pltpu.make_async_copy(out.at[at, :], result.at[at, :], sems.at[2 + half]).start()
        return carry

    lax.fori_loop(0, 2, step, 0)
    for half in range(2):
        at = slice(half * 2 * TOK, (half + 1) * 2 * TOK)
        pltpu.make_async_copy(out.at[at, :], result.at[at, :], sems.at[2 + half]).wait()


def row_part(held, norms, packets):
    pairs = 4 * TOK * 4096
    return pl.pallas_call(
        row_kernel,
        out_shape=pltpu.HBM((4 * TOK, 128), F32),
        in_specs=whole(2) + KEY_SPECS,
        out_specs=HBM,
        scratch_shapes=[pltpu.VMEM((4 * TOK, 128), F32)] * 3 + KEY_SCRATCH,
        compiler_params=PARAMS,
        cost_estimate=pl.CostEstimate(flops=2 * pairs * 640, bytes_accessed=pairs * 4, transcendentals=2 * pairs),
        name="row_part",
    )(held, norms, *as_operands(packets))


def col_kernel(query_at, place_ref, held, stat_ref, *refs):
    row_ref, keep, give = refs[8:11]
    acc, rows, late, sems = refs[-4:]
    if len(refs) == 16:
        total = jnp.sum(stat_ref[:, 0, 4 * TOK :], axis=0, keepdims=True)
        refs[11][...] = jnp.broadcast_to(total[None], (16, 1, 128))
    keys = Keys(held, refs[:8], late, sems)
    keys.start()
    at = slice(query_at, query_at + 2 * TOK)
    copy = pltpu.make_async_copy(row_ref.at[at, :], rows, sems.at[2])
    copy.start()
    toward = jnp.where(place_ref[0] == 0, 7, 1)
    for slot in range(8):
        if slot == 6:
            keys.wait()
            copy.wait()
        source = lax.rem(place_ref[1] + toward * STEPS[slot], 8)
        if slot in (0, 5):
            t_norm, s_norm = (
                jnp.concatenate([stat_ref[source, i : i + 1, k : k + TOK] for k in (0, 2 * TOK)], axis=1)
                for i in range(2)
            )
        else:
            plane = 2 * TOK * (1 - slot % 2 if slot < 5 else slot % 2)
            t_norm, s_norm = (stat_ref[source, i : i + 1, plane : plane + 2 * TOK] for i in range(2))
        stud = keys.block(slot, STUD)
        t = nt_dot(held[at, TEACH], keys.block(slot, TEACH)) * CT
        s = nt_dot(held[at, STUD], stud) * CS
        p = slopes_of(t, s, t_norm, s_norm).astype(BF16)
        part = jnp.dot(p, stud, preferred_element_type=F32)
        acc[...] = part if slot == 0 else acc[...] + part
    for i, out in enumerate((keep, give)):
        part = slice(i * TOK, (i + 1) * TOK)
        out[...] = (acc[part, :] + rows[part, :]).T[:SW, :] * (1.0 / math.sqrt(SW))


def col_part(place, held, stats, packets, rows, query_at, with_loss):
    pairs = 2 * TOK * 4096
    part = jax.ShapeDtypeStruct((SW, TOK), F32)
    return pl.pallas_call(
        functools.partial(col_kernel, query_at),
        out_shape=(part, part) + with_loss * (jax.ShapeDtypeStruct((16, 1, 128), F32),),
        in_specs=[SCALAR] + whole(2) + KEY_SPECS + [HBM],
        out_specs=tuple(whole(2 + with_loss)),
        scratch_shapes=[pltpu.VMEM((2 * TOK, 128), F32)] * 2 + KEY_SCRATCH,
        compiler_params=PARAMS,
        cost_estimate=pl.CostEstimate(flops=2 * pairs * 640, bytes_accessed=pairs * 4, transcendentals=2 * pairs),
        name="col_part",
    )(place, held, stats, *as_operands(packets), in_hbm(rows))


def onward(array):
    pairs = [(2 * z + c, 2 * ((z + (-1) ** c) % 8) + c) for z in range(8) for c in range(2)]
    return lax.ppermute(array, ("z", "c"), pairs)


def tied(*arrays):
    return lax.optimization_barrier(arrays)


def swap(array, axis):
    n = 4 if isinstance(axis, tuple) else 2
    return lax.ppermute(array, axis, [(i, n - 1 - i) for i in range(n)])


def local(teacher, student, weights):
    yl, z, c = lax.axis_index("yl"), lax.axis_index("z"), lax.axis_index("c")
    own, give = prepare(yl.reshape(1), teacher[0], student[0].T, weights.reshape(1, TOK))
    got = swap(give, "yl")
    own_pair = pair_up(own, swap(own, "c"))
    a1 = onward(own_pair)
    got_pair = pair_up(got, swap(got, "c"))
    a1, sent_pair = tied(a1, got_pair)
    b1 = onward(sent_pair)
    a2 = onward(a1)
    state, held, weight = first_stats(own_pair, got_pair)
    b1, state = tied(b1, state)
    b2 = onward(b1)
    state = more_stats(held, a1, state)
    a2, state = tied(a2, state)
    a3 = onward(a2)
    state = more_stats(held, b1, state)
    b2, state = tied(b2, state)
    b3 = onward(b2)
    state = more_stats(held, a2, state)
    a3, state = tied(a3, state)
    a4 = onward(a3[:TOK])
    state = more_stats(held, b2, state)
    b3, state = tied(b3, state)
    b4 = onward(b3[:TOK])
    for packets in (a3, b3, a4):
        state = more_stats(held, packets, state)
    state = more_stats(held, b4, state, last=True)
    packets = (a2, b2, a3, b3, a4, b4, a1, b1)
    norms, send = merge(state, swap(state, "c"), weight)
    stats = lax.all_to_all(send, "z", 0, 0, tiled=True)
    rows = row_part(held, norms, packets)
    place = jnp.stack([c, z])
    far_keep, far_give, loss = col_part(place, held, stats, packets, rows, 2 * TOK, True)
    losses = lax.all_to_all(loss, ("yl", *HEAD), 0, 0, tiled=True)
    other = swap(far_keep, "yl") + swap(far_give, ("yl", "c"))
    rows, other = tied(rows, other)
    near_keep, near_give = col_part(place, held, stats, packets, rows, 0, False)
    mine = near_keep + swap(near_give, "c")
    grad = jnp.where(yl == 0, jnp.concatenate([mine, other]), jnp.concatenate([other, mine]))
    mean_loss = jnp.sum(losses[:, 0, 0]) * (math.log(2.0) / (HEADS * 8192))
    return mean_loss, grad.T[None]


def solution(mesh):
    finer = Mesh(mesh.devices.reshape(2, 8, 2, 2, 4), ("yl", "z", "c", "yh", "x"))
    return jax.shard_map(
        local,
        mesh=finer,
        in_specs=(P(None, SEQ, HEAD), P(None, SEQ, HEAD), P(SEQ)),
        out_specs=(P(), P(None, SEQ, HEAD)),
        check_vma=False,
    )
```
